128 devices in a mesh: slab: 16 (over z, y), pencil: 8 (over x, core).
Axes of the slice: x: 4, y: 4, z: 4, core: 2. Of those that a mesh axis runs over, the one named last changes fastest.
Arguments:
- fine_density: float32 [16, 8, 8, 64, 64, 64], P('slab', 'pencil'), may hold values from 0.1 to 10
- coarse_density: float32 [1536, 512, 128], P('slab', 'pencil'), may hold values from 0.1 to 10
- patch_anchor: int32 [16, 8, 8, 3], P('slab', 'pencil'), may hold values from 0 to 96, as said below
- patch_extent: int32 [16, 8, 8, 3], P('slab', 'pencil'), may hold values from 16 to 64, as said below
- patch_owner: int32 [16, 8, 8, 1], P('slab', 'pencil'), may hold values from 0 to 15; in each aligned block of 8 rows (0 to 7, 8 to 15, ..., all dimensions but the last counted through in order) no two rows name the same one
- patch_count: int32 [16, 8], P('slab', 'pencil'), may hold values from 6 to 8, as said below
Outputs:
- potential: float32 [1536, 512, 128], P('slab', 'pencil')
- gradient: float32 [3, 1536, 512, 128], P(None, 'slab', 'pencil')
The draws below stay inside these ranges and needn't reach their ends.
Inputs may be any that keep to these rules, and one draw needn't show every extreme that they name: `patch_anchor`: component 0 lies in 0 to 64, component 1 in 0 to 32, component 2 in 0 to 96. `patch_extent`: even numbers. `patch_owner`: within the 8 slots of one device no two name the same slab. `patch_count`: some device has all 8 slots live.
All inputs are finite; a program needn't handle non-finite values.
Results may differ from the reference program's by a relative error of at most 0.0001.
Values sent between devices are 32-bit elements; how exact they have to be, the bound alone decides.
No kernel may reach another device: no remote copies, remote signals or barrier semaphores. Data moves between devices by JAX's collectives and lax.ppermute only.
A program may use at most 384 MiB of HBM per device.

```python
import math
import jax
import jax.numpy as jnp
import numpy as np
from jax import lax

CX = 96
CY = 64
NZ = 128
PB = 32
ITERS = 4
P_DEV = 8
NX = 1536
NY = 512
N_SLAB = 16
N_PENCIL = 8


def draw_patch_anchor(key, part):
    key = jax.random.fold_in(key, 11)
    shape_here = (N_SLAB, N_PENCIL, P_DEV)
    along_x = jax.random.randint(jax.random.fold_in(key, 1), shape_here, 0, CX - PB + 1)
    along_y = jax.random.randint(jax.random.fold_in(key, 2), shape_here, 0, CY - PB + 1)
    along_z = jax.random.randint(jax.random.fold_in(key, 3), shape_here, 0, NZ - PB + 1)
    return jnp.stack([along_x, along_y, along_z], axis=-1).astype(jnp.int32)


def draw_patch_extent(key, part):
    key = jax.random.fold_in(key, 23)
    halves = jax.random.randint(key, (N_SLAB, N_PENCIL, P_DEV, 3), PB // 4, PB + 1)
    return (2 * halves).astype(jnp.int32)


def draw_patch_count(key, part):
    key = jax.random.fold_in(key, 37)
    counts = jax.random.randint(key, (N_SLAB * N_PENCIL,), P_DEV - P_DEV // 4, P_DEV + 1)
    chosen = jax.random.randint(jax.random.fold_in(key, 5), (), 0, N_SLAB * N_PENCIL)
    counts = jnp.where(jnp.arange(N_SLAB * N_PENCIL) == chosen, P_DEV, counts)
    return counts.reshape(N_SLAB, N_PENCIL).astype(jnp.int32)


def levels(key, dims, shards, low, high):
    gain = 1.0
    for dim, shards_of in shards:
        steps = jax.random.uniform(jax.random.fold_in(jax.random.fold_in(key, 6), dim), (shards_of,), jnp.float32, low / len(shards), high / len(shards))
        gain = gain * jnp.repeat(jnp.exp(steps), dims[dim] // shards_of).reshape((-1,) + (1,) * (len(dims) - 1 - dim))
    return gain


def assign_block(stream_key, own, number, rows, number_of, top, most, lean):
    sequence = jax.random.permutation(stream_key, number_of)
    crowded, usual = load_shares(number_of, rows * top, most, lean, True), load_shares(number_of, rows * top, most, lean, False)
    places = jnp.arange(number_of)

    def named(lengths, offset_by):
        used = int((lengths > 0).sum())
        fixed = max(1, used // 4)
        shifted = fixed + (places - fixed + offset_by * (used - fixed)) % max(1, number_of - fixed)
        return jnp.zeros((number_of,), jnp.int32).at[sequence[jnp.where(places < fixed, places, shifted)]].set(jnp.asarray(lengths, jnp.int32))

    lengths = jnp.where(number % 4 == 0, named(crowded, number // 4), named(usual, number - number // 4 - 1))
    mixed = jax.random.permutation(jax.random.fold_in(own, 3), number_of)
    giver, receiver = mixed[0:number_of // 2 * 2:2], mixed[1:number_of // 2 * 2:2]
    margin = jnp.minimum(lengths[giver] - 1, most - lengths[receiver]) // 2
    margin = jnp.where((giver == sequence[0]) | (receiver == sequence[0]) | (lengths[receiver] == 0), 0, jnp.maximum(margin, 0))
    shifted = jax.random.randint(jax.random.fold_in(own, 4), (number_of // 2,), 0, 1 << 20) % (margin + 1)
    lengths = lengths.at[giver].add(-shifted).at[receiver].add(shifted)
    members = jnp.searchsorted(jnp.cumsum(lengths), jnp.arange(rows * top), side="right").astype(jnp.int32)
    table = members.reshape(top, rows).T
    table = table[jax.random.permutation(jax.random.fold_in(own, 1), rows)]
    offset_by = jax.random.randint(jax.random.fold_in(own, 2), (rows, 1), 0, top)
    return jnp.take_along_axis(table, (jnp.arange(top)[None, :] + offset_by) % top, axis=1)


def load_shares(count, total, limit, slope, full):
    weights = [(1 << 20) // math.isqrt(standing ** slope) + 1 for standing in range(1, count + 1)]
    largest = limit if full else min(limit, max(-(-total // count), total * weights[0] // sum(weights)))
    least = 1 if total - largest >= count - 1 else 0
    given, spare = [largest] + [least] * (count - 1), total - largest - least * (count - 1)
    while spare > 0:
        free = [i for i in range(1, count) if given[i] < largest] or [i for i in range(1, count) if given[i] < limit]
        mass, remaining = sum([weights[i] for i in free]), spare
        for i in free:
            addition = min(limit - given[i], max(1, remaining * weights[i] // mass), spare)
            given[i] = given[i] + addition
            spare = spare - addition
    return np.array(given)


def setup_inputs(seed: int = 0) -> dict:
    arg_keys = jax.random.split(jax.random.key(seed), 7)
    fine_density = jnp.clip(jnp.exp(math.log(10.0) - 4.6051702 * jax.random.uniform(arg_keys[0], (N_SLAB, N_PENCIL, P_DEV, 2 * PB, 2 * PB, 2 * PB), jnp.float32) ** levels(arg_keys[0], (N_SLAB, N_PENCIL, P_DEV, 2 * PB, 2 * PB, 2 * PB), ((0, 16), (1, 8)), -0.2, 0.2)), 0.1, 10.0)
    coarse_density = jnp.clip(jnp.exp(math.log(10.0) - 4.6051702 * jax.random.uniform(arg_keys[1], (NX, NY, NZ), jnp.float32) ** levels(arg_keys[1], (NX, NY, NZ), ((0, 16), (1, 8)), -0.2, 0.2)), 0.1, 10.0)
    patch_anchor = draw_patch_anchor(jax.random.fold_in(arg_keys[6], 71), 0)
    patch_extent = draw_patch_extent(jax.random.fold_in(arg_keys[6], 71), 0)
    patch_owner_keys = jax.random.split(jax.random.fold_in(arg_keys[4], 1), N_SLAB * N_PENCIL * P_DEV // P_DEV)
    patch_owner_turns = jax.random.permutation(jax.random.fold_in(arg_keys[4], 3), N_SLAB * N_PENCIL * P_DEV // P_DEV)
    patch_owner = jax.vmap(lambda own, number: assign_block(jax.random.fold_in(arg_keys[4], 2), own, number, P_DEV, N_SLAB, 1, 1, 0))(patch_owner_keys, patch_owner_turns).reshape((N_SLAB, N_PENCIL, P_DEV, 1))
    patch_count = draw_patch_count(jax.random.fold_in(arg_keys[6], 71), 0)
    return {"fine_density": fine_density, "coarse_density": coarse_density, "patch_anchor": patch_anchor, "patch_extent": patch_extent, "patch_owner": patch_owner, "patch_count": patch_count}


OMEGA_SIXTH = 1.0 / 9.0


def neighbours(padded):
    deeper = jnp.pad(padded, ((0, 0), (0, 0), (1, 1)))
    total = deeper[2:, 1:-1, 1:-1] + deeper[:-2, 1:-1, 1:-1]
    total = total + deeper[1:-1, 2:, 1:-1] + deeper[1:-1, :-2, 1:-1]
    total = total + deeper[1:-1, 1:-1, 2:] + deeper[1:-1, 1:-1, :-2]
    return total


def central_gradient(padded):
    deeper = jnp.pad(padded, ((0, 0), (0, 0), (1, 1)))
    grad_x = (deeper[2:, 1:-1, 1:-1] - deeper[:-2, 1:-1, 1:-1]) * 0.5
    grad_y = (deeper[1:-1, 2:, 1:-1] - deeper[1:-1, :-2, 1:-1]) * 0.5
    grad_z = (deeper[1:-1, 1:-1, 2:] - deeper[1:-1, 1:-1, :-2]) * 0.5
    return jnp.stack([grad_x, grad_y, grad_z])


def reference(fine_density, coarse_density, patch_anchor, patch_extent, patch_owner, patch_count):
    total_slots = N_SLAB * N_PENCIL * P_DEV
    fine_rows = fine_density.reshape(total_slots, 2 * PB, 2 * PB, 2 * PB)
    anchors = patch_anchor.reshape(total_slots, 3).astype(jnp.int32)
    half_size = (patch_extent.reshape(total_slots, 3) // 2).astype(jnp.int32)
    owners = patch_owner.reshape(total_slots).astype(jnp.int32)
    counts = patch_count.reshape(N_SLAB * N_PENCIL).astype(jnp.int32)
    positions = jnp.arange(PB, dtype=jnp.int32)

    def deposit(slot, source):
        slot = slot.astype(jnp.int32)
        holder = slot // P_DEV
        pencil_index = holder % N_PENCIL
        alive_mask = (slot % P_DEV < counts[holder]).astype(jnp.float32)
        patch_fine = lax.dynamic_index_in_dim(fine_rows, slot, 0, keepdims=False)
        averaged = patch_fine.reshape(PB, 2, PB, 2, PB, 2).sum(axis=(1, 3, 5)) * 0.125
        sizes_here = half_size[slot]
        covered = ((positions[:, None, None] < sizes_here[0]) & (positions[None, :, None] < sizes_here[1])
                   & (positions[None, None, :] < sizes_here[2])).astype(jnp.float32) * alive_mask
        corner_x = owners[slot] * CX + anchors[slot, 0]
        corner_y = pencil_index * CY + anchors[slot, 1]
        corner_z = anchors[slot, 2]
        density_here = lax.dynamic_slice(coarse_density, (corner_x, corner_y, corner_z), (PB, PB, PB))
        current = lax.dynamic_slice(source, (corner_x, corner_y, corner_z), (PB, PB, PB))
        coarse_block = averaged * covered
        updated = current + (coarse_block - covered * density_here)
        return lax.dynamic_update_slice(source, updated, (corner_x, corner_y, corner_z))

    source = lax.fori_loop(0, total_slots, deposit, jnp.zeros((NX, NY, NZ), jnp.float32))
    potential = OMEGA_SIXTH * source
    for sweep_index in range(ITERS - 1):
        padded = jnp.pad(potential, ((1, 1), (1, 1), (0, 0)))
        potential = potential + OMEGA_SIXTH * (source - (6.0 * potential - neighbours(padded)))
    padded = jnp.pad(potential, ((1, 1), (1, 1), (0, 0)))
    return potential, central_gradient(padded)
```

```python
import functools

import jax
import jax.numpy as jnp
from jax import lax
from jax.experimental import pallas as pl
from jax.experimental.pallas import tpu as pltpu
from jax.sharding import PartitionSpec as P

HALO = 4
META_ROWS = 8
STEP = 8
F32 = jnp.float32


def average_kernel(meta, fine, sent, packed, blank, sems, blank_sem):
    slots = pl.num_programs(0)
    p = pl.program_id(0)
    buffer = lax.rem(p, 2)
    rows = packed.shape[1] - META_ROWS
    edge = fine.shape[3] // 2
    lanes = packed.shape[2]
    groups = lanes // edge
    tiles = edge // groups
    width = fine.shape[5]

    def blank_copy():
        return pltpu.make_async_copy(blank, sent.at[:, pl.ds(rows, META_ROWS), :], blank_sem)

    def slot_copy(patch, which):
        owner = meta[6 * slots + patch]
        return pltpu.make_async_copy(packed.at[which], sent.at[owner], sems.at[which])

    @pl.when(p == 0)
    def _():
        blank[...] = jnp.zeros_like(blank)
        blank_copy().start()

    @pl.when(p >= 2)
    def _():
        slot_copy(p - 2, buffer).wait()

    total = jnp.zeros((rows, lanes), F32)
    for g in range(groups):
        part = None
        for dx in range(2):
            for dy in range(2):
                piece = fine[0, 0, 0, pl.ds(2 * g + dx, tiles, stride=2 * groups), pl.ds(dy, edge, stride=2), :]
                part = piece if part is None else part + piece
        part = part.reshape(rows, width)
        high = part.astype(jnp.bfloat16)
        low = (part - high.astype(F32)).astype(jnp.bfloat16)
        source_lane = lax.broadcasted_iota(jnp.int32, (width, lanes), 0)
        target_lane = lax.broadcasted_iota(jnp.int32, (width, lanes), 1)
        gather = jnp.where(target_lane == g * edge + source_lane // 2, 0.125, 0.0).astype(jnp.bfloat16)
        total = total + jnp.dot(high, gather, preferred_element_type=F32)
        total = total + jnp.dot(low, gather, preferred_element_type=F32)
    packed[buffer, :rows, :] = total
    lane = lax.broadcasted_iota(jnp.int32, (META_ROWS, lanes), 1)
    alive = (p < meta[7 * slots]).astype(jnp.int32)
    words = jnp.where(lane == 0, alive, 0)
    for d in range(3):
        words = jnp.where(lane == 1 + d, meta[3 * p + d], words)
        words = jnp.where(lane == 4 + d, lax.shift_right_logical(meta[3 * (slots + p) + d], 1), words)
    packed[buffer, pl.ds(rows, META_ROWS), :] = words.astype(F32)

    @pl.when(p == 0)
    def _():
        blank_copy().wait()

    slot_copy(p, buffer).start()

    @pl.when(p == slots - 1)
    def _():
        slot_copy(p - 1, 1 - buffer).wait()
        slot_copy(p, buffer).wait()


def average(fine, meta, slabs):
    slots, fine_edge = fine.shape[2], fine.shape[3]
    edge = fine_edge // 2
    rows = edge * edge * edge // 128
    block = (1, 1, 1) + fine.shape[3:]
    return pl.pallas_call(
        average_kernel,
        out_shape=jax.ShapeDtypeStruct((slabs, rows + META_ROWS, 128), F32),
        grid_spec=pltpu.PrefetchScalarGridSpec(
            num_scalar_prefetch=1,
            grid=(slots,),
            in_specs=[pl.BlockSpec(block, lambda p, meta: (0, 0, p, 0, 0, 0))],
            out_specs=pl.BlockSpec(memory_space=pl.ANY),
            scratch_shapes=[
                pltpu.VMEM((2, rows + META_ROWS, 128), F32),
                pltpu.VMEM((slabs, META_ROWS, 128), F32),
                pltpu.SemaphoreType.DMA((2,)),
                pltpu.SemaphoreType.DMA,
            ],
        ),
        compiler_params=pltpu.CompilerParams(
            dimension_semantics=("arbitrary",), vmem_limit_bytes=32 << 20
        ),
        name="average",
    )(meta, fine)


def deposit_kernel(received, coarse, source, y_low, y_high, words, sem):
    slabs, all_rows, lanes = received.shape
    rows = all_rows - META_ROWS
    edge = 32
    groups = lanes // edge
    planes, height, _ = source.shape
    for s in range(slabs):
        pltpu.make_async_copy(received.at[s, rows], words.at[s], sem).start()
    source[...] = jnp.zeros_like(source)
    for s in range(slabs):
        pltpu.make_async_copy(received.at[s, rows], words.at[s], sem).wait()
    row = lax.broadcasted_iota(jnp.int32, (edge, lanes), 0)
    lane = lax.broadcasted_iota(jnp.int32, (edge, lanes), 1)

    @pl.loop(0, slabs)
    def _(s):
        word = lambda k: words[s, k].astype(jnp.int32)

        @pl.when(word(0) > 0)
        def _():
            ax, ay, az, hx, hy, hz = (word(k) for k in range(1, 7))
            covered = (row < hy) & (lane >= az) & (lane < az + hz)
            here = pl.ds(ay, edge)

            @pl.loop(0, lax.shift_right_logical(hx + groups - 1, 2))
            def _(tile):
                data = received[s, pl.ds(pl.multiple_of(tile * edge, edge), edge), :]
                for g in range(groups):
                    i = tile * groups + g
                    x = ax + i
                    moved = pltpu.roll(data, lax.rem(az + lanes - g * edge, lanes), 1)
                    change = jnp.where(covered & (i < hx), moved - coarse[x, here, :], 0.0)
                    source[x, here, :] = source[x, here, :] + change

    @pl.loop(0, planes // 2)
    def _(k):
        for half in range(2):
            y_low[k, half * HALO : half * HALO + HALO, :] = source[2 * k + half, 0:HALO, :]
            y_high[k, half * HALO : half * HALO + HALO, :] = source[2 * k + half, height - HALO : height, :]


def deposit(received, coarse):
    planes, height, lanes = coarse.shape
    face = jax.ShapeDtypeStruct((planes // 2, 2 * HALO, lanes), F32)
    vmem = pl.BlockSpec(memory_space=pltpu.VMEM)
    return pl.pallas_call(
        deposit_kernel,
        out_shape=[jax.ShapeDtypeStruct(coarse.shape, F32), face, face],
        in_specs=[vmem, vmem],
        out_specs=[vmem, vmem, vmem],
        scratch_shapes=[pltpu.SMEM((received.shape[0], lanes), F32), pltpu.SemaphoreType.DMA],
        compiler_params=pltpu.CompilerParams(vmem_limit_bytes=32 << 20),
        name="deposit",
    )(received, coarse)


def sweep_kernel(slabs, pencils, place, source, y_low, y_high, x_low, x_high, potential, gradient,
                 q1, q2, q3, q4, sems):
    step = pl.program_id(0)
    steps = pl.num_programs(0)
    planes, height, lanes = source.shape
    first, last = place[0] == 0, place[0] == slabs - 1
    left, right = place[1] == 0, place[1] == pencils - 1
    top = HALO + planes
    base = 2 * HALO
    window = pl.ds(HALO, height + 2 * HALO)
    below = pl.ds(HALO - 1, height + 2 * HALO)
    above = pl.ds(HALO + 1, height + 2 * HALO)

    def chunk(c):
        start = c * STEP if isinstance(c, int) else pl.multiple_of(c * STEP, STEP)
        return pltpu.make_async_copy(
            source.at[pl.ds(start, STEP)],
            q1.at[pl.ds(HALO + start, STEP), pl.ds(base, height), :],
            sems.at[c],
        )

    row = lax.broadcasted_iota(jnp.int32, (8, lanes), 0)
    keep_low = jnp.where(left & (row < HALO), 0.0, 1.0)
    keep_high = jnp.where(right & (row >= HALO), 0.0, 1.0)
    lane = lax.broadcasted_iota(jnp.int32, (height, lanes), 1)

    @pl.when(step == 0)
    def _():
        for c in range(planes // STEP):
            chunk(c).start()

        @pl.loop(0, planes // 2)
        def _(k):
            low = jnp.where(left, 0.0, y_low[k])
            high = jnp.where(right, 0.0, y_high[k])
            for half in range(2):
                x = HALO + 2 * k + half
                q1[x, HALO:base, :] = low[half * HALO : half * HALO + HALO]
                q1[x, base + height : base + height + HALO, :] = high[half * HALO : half * HALO + HALO]

        zero = jnp.zeros((height + 2 * HALO, lanes), F32)
        for i in range(HALO):
            for edge, x, face in ((first, i, x_low), (last, top + i, x_high)):
                value = jnp.where(edge, 0.0, face[i])
                q1[x, HALO : HALO + 8, :] = value[:8] * keep_low
                q1[x, HALO + 8 : height + HALO, :] = value[8:height]
                q1[x, height + HALO : height + 2 * HALO + HALO, :] = value[height:] * keep_high
                for q in (q2, q3, q4):
                    q[x, window, :] = zero
        chunk(0).wait()

    @pl.when(step < steps - 1)
    def _():
        chunk(step + 1).wait()

    def sides(value):
        lane_here = lax.broadcasted_iota(jnp.int32, value.shape, 1)
        down = jnp.where(lane_here == 0, 0.0, pltpu.roll(value, 1, 1))
        up = jnp.where(lane_here == lanes - 1, 0.0, pltpu.roll(value, lanes - 1, 1))
        return down, up

    def sweep(old, new, low, high):
        def body(x, carry):
            before, here = carry
            after = old[x + 1, window, :]
            down, up = sides(here)
            around = (before + after) + (old[x, below, :] + old[x, above, :]) + (down + up)
            value = q1[x, window, :] + (3.0 * here + around) * (1.0 / 9.0)
            new[x, HALO : HALO + 8, :] = value[:8] * keep_low
            new[x, HALO + 8 : height + HALO, :] = value[8:height]
            new[x, height + HALO : height + 2 * HALO + HALO, :] = value[height:] * keep_high
            return here, after

        lax.fori_loop(low, high, body, (old[low - 1, window, :], old[low, window, :]))

    for k, (old, new) in enumerate(((q1, q2), (q2, q3), (q3, q4))):
        start = jnp.where(step == 0, jnp.where(first, HALO, 1 + k), 7 - k + STEP * step)
        stop = jnp.minimum(15 - k + STEP * step, jnp.where(last, top, top + HALO - 1 - k))
        sweep(old, new, start, stop)

    own = pl.ds(base, height)

    def finish(j, carry):
        before, here = carry
        x = HALO + STEP * step + j
        after = q4[x + 1, own, :]
        down, up = sides(here)
        potential[j] = here * (1.0 / 9.0)
        gradient[0, j] = (after - before) * (0.5 / 9.0)
        gradient[1, j] = (q4[x, pl.ds(base + 1, height), :] - q4[x, pl.ds(base - 1, height), :]) * (0.5 / 9.0)
        gradient[2, j] = (up - down) * (0.5 / 9.0)
        return here, after

    x0 = HALO + STEP * step
    lax.fori_loop(0, STEP, finish, (q4[x0 - 1, own, :], q4[x0, own, :]))


def sweeps(place, source, y_low, y_high, x_low, x_high, slabs, pencils):
    planes, height, lanes = source.shape
    whole = lambda a: pl.BlockSpec(a.shape, lambda i, place: (0,) * a.ndim)
    field = pltpu.VMEM((planes + 2 * HALO, height + 4 * HALO, lanes), F32)
    return pl.pallas_call(
        functools.partial(sweep_kernel, slabs, pencils),
        out_shape=[
            jax.ShapeDtypeStruct(source.shape, F32),
            jax.ShapeDtypeStruct((3,) + source.shape, F32),
        ],
        grid_spec=pltpu.PrefetchScalarGridSpec(
            num_scalar_prefetch=1,
            grid=(planes // STEP,),
            in_specs=[pl.BlockSpec(memory_space=pl.ANY)] + [whole(a) for a in (y_low, y_high, x_low, x_high)],
            out_specs=[
                pl.BlockSpec((STEP, height, lanes), lambda i, place: (i, 0, 0)),
                pl.BlockSpec((3, STEP, height, lanes), lambda i, place: (0, i, 0, 0)),
            ],
            scratch_shapes=[field, field, field, field, pltpu.SemaphoreType.DMA((planes // STEP,))],
        ),
        compiler_params=pltpu.CompilerParams(
            dimension_semantics=("arbitrary",), vmem_limit_bytes=48 << 20
        ),
        name="sweeps",
    )(place, source, y_low, y_high, x_low, x_high)


def ring(values, axis, count):
    up = [(i, (i + 1) % count) for i in range(count)]
    down = [((i + 1) % count, i) for i in range(count)]
    low, high = values
    return lax.ppermute(high, axis, up), lax.ppermute(low, axis, down)


def on_device(fine, coarse, anchor, extent, owner, count):
    slabs, pencils = lax.axis_size("slab"), lax.axis_size("pencil")
    meta = jnp.concatenate(
        [anchor.reshape(-1), extent.reshape(-1), owner.reshape(-1), count.reshape(-1)]
    )
    sent = average(fine, meta, slabs)
    received = lax.all_to_all(sent, "slab", split_axis=0, concat_axis=0, tiled=True)
    source, y_low, y_high = deposit(received, coarse)
    planes, height, lanes = source.shape
    y_low, y_high = ring((y_low, y_high), "pencil", pencils)

    def face(at):
        near = slice(at // 2, at // 2 + HALO // 2)
        return jnp.concatenate(
            [y_low[near].reshape(HALO, HALO, lanes), source[at : at + HALO],
             y_high[near].reshape(HALO, HALO, lanes)],
            axis=1,
        )

    x_low, x_high = ring((face(0), face(planes - HALO)), "slab", slabs)
    place = jnp.stack([lax.axis_index("slab"), lax.axis_index("pencil")]).astype(jnp.int32)
    potential, gradient = sweeps(place, source, y_low, y_high, x_low, x_high, slabs, pencils)
    return potential, gradient


def solution(mesh):
    in_specs = (
        P("slab", "pencil", None, None, None, None),
        P("slab", "pencil", None),
        P("slab", "pencil", None, None),
        P("slab", "pencil", None, None),
        P("slab", "pencil", None, None),
        P("slab", "pencil"),
    )
    out_specs = (P("slab", "pencil", None), P(None, "slab", "pencil", None))
    return jax.shard_map(
        on_device, mesh=mesh, in_specs=in_specs, out_specs=out_specs, check_vma=False
    )
```

```python
import functools

import jax
import jax.numpy as jnp
from jax import lax
from jax.experimental import pallas as pl
from jax.experimental.pallas import tpu as pltpu
from jax.sharding import PartitionSpec as P

HALO = 4
META_ROWS = 8
STEP = 8
BASE = 8
F32 = jnp.float32


def average_kernel(anchor, extent, owners, count, fine, sent, cells, packed, blank, in_sems, out_sem, blank_sem):
    slots, fine_edge = cells.shape[:2]
    rows = packed.shape[1] - META_ROWS
    edge = fine_edge // 2
    lanes = packed.shape[2]
    groups = lanes // edge
    tiles = edge // groups
    parts = in_sems.shape[1]
    share = fine_edge // parts

    def load(p, part):
        here = pl.ds(part * share, share)
        return pltpu.make_async_copy(fine.at[0, 0, p, here], cells.at[p, here], in_sems.at[p, part])

    def store(p):
        return pltpu.make_async_copy(packed.at[p], sent.at[owners[0, 0, 0, p]], out_sem)

    def clear():
        return pltpu.make_async_copy(blank, sent.at[:, pl.ds(rows, META_ROWS), :], blank_sem)

    for p in range(slots):
        for part in range(parts):
            load(p, part).start()
    blank[...] = jnp.zeros_like(blank)
    clear().start()
    lane = lax.broadcasted_iota(jnp.int32, (META_ROWS, lanes), 1)
    source_lane = lax.broadcasted_iota(jnp.int32, (fine_edge, lanes), 0)
    target_lane = lax.broadcasted_iota(jnp.int32, (fine_edge, lanes), 1)

    @pl.loop(0, slots)
    def _(p):
        for part in range(parts):
            load(p, part).wait()
        total = jnp.zeros((rows, lanes), F32)
        for g in range(groups):
            pieces = [
                cells[p, pl.ds(2 * g + dx, tiles, stride=2 * groups), pl.ds(dy, edge, stride=2), :]
                for dx in range(2) for dy in range(2)
            ]
            part = ((pieces[0] + pieces[1]) + (pieces[2] + pieces[3])).reshape(rows, fine_edge)
            high = part.astype(jnp.bfloat16)
            low = (part - high.astype(F32)).astype(jnp.bfloat16)
            gather = jnp.where(target_lane == g * edge + source_lane // 2, 0.125, 0.0).astype(jnp.bfloat16)
            total = total + jnp.dot(high, gather, preferred_element_type=F32)
            total = total + jnp.dot(low, gather, preferred_element_type=F32)
        packed[p, :rows, :] = total
        alive = (p < count[0, 0]).astype(jnp.int32)
        words = jnp.where(lane == 0, alive, 0)
        for d in range(3):
            words = jnp.where(lane == 1 + d, anchor[0, d, 0, p], words)
            words = jnp.where(lane == 4 + d, lax.shift_right_logical(extent[0, d, 0, p], 1), words)
        packed[p, pl.ds(rows, META_ROWS), :] = words.astype(F32)
        pl.when(p == 0)(lambda: clear().wait())
        store(p).start()

    @pl.loop(0, slots)
    def _(p):
        store(p).wait()


def average(fine, anchor, extent, owner, count, slabs):
    by_component = lambda a: jnp.transpose(a, (0, 3, 1, 2))
    slots, fine_edge = fine.shape[2], fine.shape[3]
    edge = fine_edge // 2
    rows = edge * edge * edge // 128
    smem = pl.BlockSpec(memory_space=pltpu.SMEM)
    return pl.pallas_call(
        average_kernel,
        out_shape=jax.ShapeDtypeStruct((slabs, rows + META_ROWS, 128), F32),
        in_specs=[smem, smem, smem, smem, pl.BlockSpec(memory_space=pl.ANY)],
        out_specs=pl.BlockSpec(memory_space=pl.ANY),
        scratch_shapes=[
            pltpu.VMEM(fine.shape[2:], F32),
            pltpu.VMEM((slots, rows + META_ROWS, 128), F32),
            pltpu.VMEM((slabs, META_ROWS, 128), F32),
            pltpu.SemaphoreType.DMA((slots, 2)),
            pltpu.SemaphoreType.DMA,
            pltpu.SemaphoreType.DMA,
        ],
        compiler_params=pltpu.CompilerParams(vmem_limit_bytes=56 << 20),
        name="average",
    )(by_component(anchor), by_component(extent), by_component(owner), count, fine)


def deposit_kernel(received, coarse, source, y_low, y_high, words, sem):
    slabs, all_rows, lanes = received.shape
    rows = all_rows - META_ROWS
    edge = 32
    groups = lanes // edge
    planes, height, _ = source.shape
    for s in range(slabs):
        pltpu.make_async_copy(received.at[s, rows], words.at[s], sem).start()
    source[...] = jnp.zeros_like(source)
    for s in range(slabs):
        pltpu.make_async_copy(received.at[s, rows], words.at[s], sem).wait()
    row = lax.broadcasted_iota(jnp.int32, (edge, lanes), 0)
    lane = lax.broadcasted_iota(jnp.int32, (edge, lanes), 1)

    @pl.loop(0, slabs)
    def _(s):
        word = lambda k: words[s, k].astype(jnp.int32)

        @pl.when(word(0) > 0)
        def _():
            ax, ay, az, hx, hy, hz = (word(k) for k in range(1, 7))
            covered = (row < hy) & (lane >= az) & (lane < az + hz)
            here = pl.ds(ay, edge)

            @pl.loop(0, lax.shift_right_logical(hx + groups - 1, 2))
            def _(tile):
                data = received[s, pl.ds(pl.multiple_of(tile * edge, edge), edge), :]
                for g in range(groups):
                    i = tile * groups + g
                    x = ax + i
                    moved = pltpu.roll(data, lax.rem(az + lanes - g * edge, lanes), 1)
                    change = jnp.where(covered & (i < hx), moved - coarse[x, here, :], 0.0)
                    source[x, here, :] = source[x, here, :] + change

    @pl.loop(0, planes // 2)
    def _(k):
        for half in range(2):
            y_low[k, half * HALO : half * HALO + HALO, :] = source[2 * k + half, 0:HALO, :]
            y_high[k, half * HALO : half * HALO + HALO, :] = source[2 * k + half, height - HALO : height, :]


def deposit(received, coarse):
    planes, height, lanes = coarse.shape
    face = jax.ShapeDtypeStruct((planes // 2, 2 * HALO, lanes), F32)
    vmem = pl.BlockSpec(memory_space=pltpu.VMEM)
    return pl.pallas_call(
        deposit_kernel,
        out_shape=[jax.ShapeDtypeStruct(coarse.shape, F32), face, face],
        in_specs=[vmem, vmem],
        out_specs=[vmem, vmem, vmem],
        scratch_shapes=[pltpu.SMEM((received.shape[0], lanes), F32), pltpu.SemaphoreType.DMA],
        compiler_params=pltpu.CompilerParams(vmem_limit_bytes=32 << 20),
        name="deposit",
    )(received, coarse)


def sweep_kernel(slabs, pencils, place, source, y_low, y_high, x_low, x_high, potential, gradient,
                 q1, q2, q3, q4, potential_out, gradient_out, sems):
    planes, height, lanes = source.shape
    rows = height // 8
    steps = planes // STEP
    first, last = place[0] == 0, place[0] == slabs - 1
    left, right = place[1] == 0, place[1] == pencils - 1
    row = lax.broadcasted_iota(jnp.int32, (8, lanes), 0)
    lane = lax.broadcasted_iota(jnp.int32, (8, lanes), 1)
    keep = jnp.where((right & (row < HALO)) | (left & (row >= HALO)), 0.0, 1.0)

    def send(i):
        here = pl.ds(i * STEP, STEP)
        copies = [pltpu.make_async_copy(potential_out.at[here], potential.at[here], sems.at[0])]
        for d in range(3):
            copies.append(pltpu.make_async_copy(gradient_out.at[d, here], gradient.at[d, here], sems.at[1 + d]))
        return copies

    def comb(t):
        return pl.ds(t, 8, stride=rows)

    def load(field, x):
        return tuple(field[x, t] for t in range(rows + 1))

    def unpack(c):
        for j in range(STEP):
            x = c * STEP + j
            for t in range(rows):
                q1[BASE + x, t] = source[x, comb(t), :]

    @pl.loop(0, planes // 2)
    def _(k):
        low, high = y_low[k], y_high[k]
        q1[BASE + 2 * k, rows] = jnp.where(row < HALO, high, pltpu.roll(low, HALO, 0)) * keep
        q1[BASE + 2 * k + 1, rows] = jnp.where(row < HALO, pltpu.roll(high, HALO, 0), low) * keep

    for i in range(HALO):
        for edge, x, face in ((first, BASE - HALO + i, x_low), (last, BASE + planes + i, x_high)):
            scale = jnp.where(edge, 0.0, 1.0)
            for t in range(rows):
                q1[x, t] = face[i, comb(HALO + t), :] * scale
            ends = jnp.where(row < HALO, face[i, 0:8, :], face[i, height : height + 8, :])
            q1[x, rows] = pltpu.roll(ends, HALO, 0) * (keep * scale)

    def along_z(value):
        down = jnp.where(lane == 0, 0.0, pltpu.roll(value, 1, 1))
        up = jnp.where(lane == lanes - 1, 0.0, pltpu.roll(value, lanes - 1, 1))
        return down, up

    def along_y(here):
        ends = here[rows]
        below = (pltpu.roll(jnp.where(row == 7, ends, here[rows - 1]), 1, 0),) + here[: rows - 1]
        above = here[1:rows] + (pltpu.roll(jnp.where(row == 0, ends, here[0]), 7, 0),)
        below += (pltpu.roll(jnp.where(row == 7, here[rows - 1], ends), 1, 0),)
        above += (pltpu.roll(jnp.where(row == 0, here[0], ends), 7, 0),)
        return below, above

    def sweep(old, new, start):
        before, here = load(old, start - 1), load(old, start)
        for j in range(STEP):
            x = start + j
            after = load(old, x + 1)
            below, above = along_y(here)
            for t in range(rows + 1):
                down, up = along_z(here[t])
                around = (before[t] + after[t]) + (below[t] + above[t]) + (down + up)
                value = q1[x, t] + (3.0 * here[t] + around) * (1.0 / 9.0)
                value = value * keep if t == rows else value
                new[x, t] = value
            before, here = here, after
        return value

    def clear(field, start):
        for i in range(HALO):
            field[start + i] = jnp.zeros((rows + 1, 8, lanes), F32)

    fields = ((q1, q2), (q2, q3), (q3, q4))
    unpack(0)
    for k, (old, new) in enumerate(fields):
        ends = sweep(old, new, BASE - 5 - k)
        pl.when(first)(functools.partial(clear, new, BASE - HALO))

    def advance(i, ends):
        pl.when(i < steps - 1)(lambda: unpack(i + 1))
        for k, (old, new) in enumerate(fields):
            next_ends = sweep(old, new, BASE + 3 - k + i * STEP)
            pl.when(last & (i == steps - 1))(functools.partial(clear, new, BASE + planes))
        x0 = BASE + i * STEP
        before, here = load(q4, x0 - 1), load(q4, x0)[:rows] + (ends,)
        for j in range(STEP):
            x = i * STEP + j
            after = load(q4, x0 + j + 1)
            below, above = along_y(here)
            for t in range(rows):
                down, up = along_z(here[t])
                potential_out[x, comb(t), :] = here[t] * (1.0 / 9.0)
                gradient_out[0, x, comb(t), :] = (after[t] - before[t]) * (0.5 / 9.0)
                gradient_out[1, x, comb(t), :] = (above[t] - below[t]) * (0.5 / 9.0)
                gradient_out[2, x, comb(t), :] = (up - down) * (0.5 / 9.0)
            before, here = here, after
        for copy in send(i):
            copy.start()
        return next_ends

    lax.fori_loop(0, steps, advance, ends)

    @pl.loop(0, steps)
    def _(i):
        for copy in send(i):
            copy.wait()


def sweeps(place, source, y_low, y_high, x_low, x_high, slabs, pencils):
    planes, height, lanes = source.shape
    field = pltpu.VMEM((BASE + planes + 2 * HALO, height // 8 + 1, 8, lanes), F32)
    vmem = pl.BlockSpec(memory_space=pltpu.VMEM)
    return pl.pallas_call(
        functools.partial(sweep_kernel, slabs, pencils),
        out_shape=[
            jax.ShapeDtypeStruct(source.shape, F32),
            jax.ShapeDtypeStruct((3,) + source.shape, F32),
        ],
        in_specs=[pl.BlockSpec(memory_space=pltpu.SMEM)] + [vmem] * 5,
        out_specs=[pl.BlockSpec(memory_space=pl.ANY)] * 2,
        scratch_shapes=[
            field, field, field, field,
            pltpu.VMEM(source.shape, F32),
            pltpu.VMEM((3,) + source.shape, F32),
            pltpu.SemaphoreType.DMA((4,)),
        ],
        compiler_params=pltpu.CompilerParams(vmem_limit_bytes=44 << 20),
        name="sweeps",
    )(place, source, y_low, y_high, x_low, x_high)


def ring(values, axis, count):
    up = [(i, (i + 1) % count) for i in range(count)]
    down = [((i + 1) % count, i) for i in range(count)]
    low, high = values
    return lax.ppermute(high, axis, up), lax.ppermute(low, axis, down)


def on_device(fine, coarse, anchor, extent, owner, count):
    slabs, pencils = lax.axis_size("slab"), lax.axis_size("pencil")
    sent = average(fine, anchor, extent, owner, count, slabs)
    received = lax.all_to_all(sent, "slab", split_axis=0, concat_axis=0, tiled=True)
    source, y_low, y_high = deposit(received, coarse)
    planes, height, lanes = source.shape
    y_low, y_high = ring((y_low, y_high), "pencil", pencils)

    def face(at):
        near = slice(at // 2, at // 2 + HALO // 2)
        return jnp.concatenate(
            [y_low[near].reshape(HALO, HALO, lanes), source[at : at + HALO],
             y_high[near].reshape(HALO, HALO, lanes)],
            axis=1,
        )

    x_low, x_high = ring((face(0), face(planes - HALO)), "slab", slabs)
    place = jnp.stack([lax.axis_index("slab"), lax.axis_index("pencil")]).astype(jnp.int32)
    potential, gradient = sweeps(place, source, y_low, y_high, x_low, x_high, slabs, pencils)
    return potential, gradient


def solution(mesh):
    in_specs = (
        P("slab", "pencil", None, None, None, None),
        P("slab", "pencil", None),
        P("slab", "pencil", None, None),
        P("slab", "pencil", None, None),
        P("slab", "pencil", None, None),
        P("slab", "pencil"),
    )
    out_specs = (P("slab", "pencil", None), P(None, "slab", "pencil", None))
    return jax.shard_map(
        on_device, mesh=mesh, in_specs=in_specs, out_specs=out_specs, check_vma=False
    )
```

```python
import functools

import jax
import jax.numpy as jnp
from jax import lax
from jax.experimental import pallas as pl
from jax.experimental.pallas import tpu as pltpu
from jax.sharding import PartitionSpec as P

HALO = 4
META_ROWS = 8
STEP = 8
BASE = 8
GROUP = 4
F32 = jnp.float32


def average_kernel(slab, pencil, anchor, extent, owners, count, fine, sent, cells, packed, blank, in_sems, out_sem, blank_sem):
    slots, fine_edge = cells.shape[:2]
    rows = packed.shape[1] - META_ROWS
    edge = fine_edge // 2
    lanes = packed.shape[2]
    groups = lanes // edge
    tiles = edge // groups
    parts = in_sems.shape[1]
    share = fine_edge // parts

    def load(p, part):
        here = pl.ds(part * share, share)
        return pltpu.make_async_copy(fine.at[0, 0, p, here], cells.at[p, here], in_sems.at[p, part])

    def store(p):
        return pltpu.make_async_copy(packed.at[p], sent.at[owners[0, 0, 0, p]], out_sem)

    def clear():
        return pltpu.make_async_copy(blank, sent.at[:, pl.ds(rows, META_ROWS), :], blank_sem)

    for p in range(slots):
        for part in range(parts):
            load(p, part).start()
    blank[...] = jnp.zeros_like(blank)
    clear().start()
    lane = lax.broadcasted_iota(jnp.int32, (META_ROWS, lanes), 1)
    source_lane = lax.broadcasted_iota(jnp.int32, (fine_edge, lanes), 0)
    target_lane = lax.broadcasted_iota(jnp.int32, (fine_edge, lanes), 1)

    @pl.loop(0, slots)
    def _(p):
        for part in range(parts):
            load(p, part).wait()
        total = jnp.zeros((rows, lanes), F32)
        for g in range(groups):
            pieces = [
                cells[p, pl.ds(2 * g + dx, tiles, stride=2 * groups), pl.ds(dy, edge, stride=2), :]
                for dx in range(2) for dy in range(2)
            ]
            part = ((pieces[0] + pieces[1]) + (pieces[2] + pieces[3])).reshape(rows, fine_edge)
            high = part.astype(jnp.bfloat16)
            low = (part - high.astype(F32)).astype(jnp.bfloat16)
            gather = jnp.where(target_lane == g * edge + source_lane // 2, 0.125, 0.0).astype(jnp.bfloat16)
            total = total + jnp.dot(high, gather, preferred_element_type=F32)
            total = total + jnp.dot(low, gather, preferred_element_type=F32)
        packed[p, :rows, :] = total
        alive = (p < count[0, 0]).astype(jnp.int32)
        words = jnp.where(lane == 0, alive, 0)
        for d in range(3):
            words = jnp.where(lane == 1 + d, anchor[0, d, 0, p], words)
            words = jnp.where(lane == 4 + d, lax.shift_right_logical(extent[0, d, 0, p], 1), words)
        packed[p, pl.ds(rows, META_ROWS), :] = words.astype(F32)
        pl.when(p == 0)(lambda: clear().wait())
        store(p).start()

    @pl.loop(0, slots)
    def _(p):
        store(p).wait()


def average(place, fine, anchor, extent, owner, count, slabs):
    by_component = lambda a: jnp.transpose(a, (0, 3, 1, 2))
    slots, fine_edge = fine.shape[2], fine.shape[3]
    edge = fine_edge // 2
    rows = edge * edge * edge // 128
    smem = pl.BlockSpec(memory_space=pltpu.SMEM)
    return pl.pallas_call(
        average_kernel,
        out_shape=jax.ShapeDtypeStruct((slabs, rows + META_ROWS, 128), F32),
        in_specs=[smem] * 6 + [pl.BlockSpec(memory_space=pl.ANY)],
        out_specs=pl.BlockSpec(memory_space=pl.ANY),
        scratch_shapes=[
            pltpu.VMEM(fine.shape[2:], F32),
            pltpu.VMEM((slots, rows + META_ROWS, 128), F32),
            pltpu.VMEM((slabs, META_ROWS, 128), F32),
            pltpu.SemaphoreType.DMA((slots, 2)),
            pltpu.SemaphoreType.DMA,
            pltpu.SemaphoreType.DMA,
        ],
        compiler_params=pltpu.CompilerParams(vmem_limit_bytes=56 << 20),
        name="average",
    )(*place, by_component(anchor), by_component(extent), by_component(owner), count, fine)


def deposit_kernel(received, coarse, source, y_low, y_high, words, sem):
    slabs, all_rows, lanes = received.shape
    rows = all_rows - META_ROWS
    edge = 32
    groups = lanes // edge
    planes, height, _ = source.shape
    for s in range(slabs):
        pltpu.make_async_copy(received.at[s, rows], words.at[s], sem).start()
    source[...] = jnp.zeros_like(source)
    for s in range(slabs):
        pltpu.make_async_copy(received.at[s, rows], words.at[s], sem).wait()
    row = lax.broadcasted_iota(jnp.int32, (edge, lanes), 0)
    lane = lax.broadcasted_iota(jnp.int32, (edge, lanes), 1)

    @pl.loop(0, slabs)
    def _(s):
        word = lambda k: words[s, k].astype(jnp.int32)

        @pl.when(word(0) > 0)
        def _():
            ax, ay, az, hx, hy, hz = (word(k) for k in range(1, 7))
            covered = (row < hy) & (lane >= az) & (lane < az + hz)
            here = pl.ds(ay, edge)

            @pl.loop(0, lax.shift_right_logical(hx + groups - 1, 2))
            def _(tile):
                data = received[s, pl.ds(pl.multiple_of(tile * edge, edge), edge), :]
                for g in range(groups):
                    i = tile * groups + g
                    x = ax + i
                    moved = pltpu.roll(data, lax.rem(az + lanes - g * edge, lanes), 1)
                    change = jnp.where(covered & (i < hx), moved - coarse[x, here, :], 0.0)
                    source[x, here, :] = source[x, here, :] + change

    @pl.loop(0, planes // 2)
    def _(k):
        for half in range(2):
            y_low[k, half * HALO : half * HALO + HALO, :] = source[2 * k + half, 0:HALO, :]
            y_high[k, half * HALO : half * HALO + HALO, :] = source[2 * k + half, height - HALO : height, :]


def deposit(received, coarse):
    planes, height, lanes = coarse.shape
    face = jax.ShapeDtypeStruct((planes // 2, 2 * HALO, lanes), F32)
    vmem = pl.BlockSpec(memory_space=pltpu.VMEM)
    return pl.pallas_call(
        deposit_kernel,
        out_shape=[jax.ShapeDtypeStruct(coarse.shape, F32), face, face],
        in_specs=[vmem, vmem],
        out_specs=[vmem, vmem, vmem],
        scratch_shapes=[pltpu.SMEM((received.shape[0], lanes), F32), pltpu.SemaphoreType.DMA],
        compiler_params=pltpu.CompilerParams(vmem_limit_bytes=4 << 20),
        name="deposit",
    )(received, coarse)


def along_z(value):
    lanes = value.shape[1]
    lane = lax.broadcasted_iota(jnp.int32, value.shape, 1)
    down = jnp.where(lane == 0, 0.0, pltpu.roll(value, 1, 1))
    up = jnp.where(lane == lanes - 1, 0.0, pltpu.roll(value, lanes - 1, 1))
    return down, up


def z_terms(value):
    lanes = value.shape[1]
    lane = lax.broadcasted_iota(jnp.int32, value.shape, 1)
    down = [None] + [jnp.where(lane < d, 0.0, pltpu.roll(value, d, 1)) for d in (1, 2, 3)]
    up = [None] + [jnp.where(lane >= lanes - d, 0.0, pltpu.roll(value, lanes - d, 1)) for d in (1, 2, 3)]
    outer = (lane == 0) | (lane == lanes - 1)
    once = down[1] + up[1]
    twice = (down[2] + up[2]) + jnp.where(outer, 1.0, 2.0) * value
    thrice = (down[3] + up[3]) + (
        jnp.where((lane == 0) | (lane == lanes - 2), 2.0, 3.0) * up[1]
        + jnp.where((lane == 1) | (lane == lanes - 1), 2.0, 3.0) * down[1]
    )
    return (
        value,
        value + once * (1.0 / 3.0),
        value + (once * (2.0 / 9.0) + twice * (1.0 / 27.0)),
        (value + once * (1.0 / 9.0)) + (twice * (1.0 / 81.0) + thrice * (1.0 / 729.0)),
    )


def prepare_kernel(source, *fields):
    planes, height, _ = source.shape
    rows = height // 8

    @pl.loop(0, planes // GROUP)
    def _(k):
        for j in range(GROUP):
            for t in range(rows):
                for field, term in zip(fields, z_terms(source[GROUP * k + j, pl.ds(t, 8, stride=rows), :])):
                    field[GROUP * k + j, t] = term


def prepare(source):
    planes, height, lanes = source.shape
    field = jax.ShapeDtypeStruct((planes, height // 8, 8, lanes), F32)
    vmem = pl.BlockSpec(memory_space=pltpu.VMEM)
    return pl.pallas_call(
        prepare_kernel,
        out_shape=[field] * 4,
        in_specs=[vmem],
        out_specs=[vmem] * 4,
        compiler_params=pltpu.CompilerParams(vmem_limit_bytes=4 << 20),
        cost_estimate=pl.CostEstimate(flops=1 << 25, bytes_accessed=15 << 20, transcendentals=0),
        name="prepare",
    )(source)


def y_ends(low, high, half):
    row = lax.broadcasted_iota(jnp.int32, low.shape, 0)
    if half == 0:
        return jnp.where(row < HALO, high, pltpu.roll(low, HALO, 0))
    return jnp.where(row < HALO, pltpu.roll(high, HALO, 0), low)


def faces_kernel(field, y_low, y_high, x_low, x_high):
    planes, rows, _, _ = field.shape
    for face, start in ((x_low, 0), (x_high, planes - HALO)):
        for i in range(HALO):
            k, half = divmod(start + i, 2)
            for t in range(rows):
                face[i, t] = field[start + i, t]
            face[i, rows] = y_ends(y_low[k], y_high[k], half)


def faces(field, y_low, y_high):
    face = jax.ShapeDtypeStruct((HALO, field.shape[1] + 1) + field.shape[2:], F32)
    vmem = pl.BlockSpec(memory_space=pltpu.VMEM)
    return pl.pallas_call(
        faces_kernel,
        out_shape=[face, face],
        in_specs=[vmem] * 3,
        out_specs=[vmem] * 2,
        compiler_params=pltpu.CompilerParams(vmem_limit_bytes=4 << 20),
        name="faces",
    )(field, y_low, y_high)


def sweep_kernel(inner, slabs, pencils, slab, pencil, f0, f1, f2, f3, y_low, y_high, *rest):
    if inner:
        potential, gradient, *rest = rest
    else:
        x_low, x_high, _, _, potential, gradient, *rest = rest
    ends, v1, v2, v3, potential_out, gradient_out, sems, *rest = rest
    fields = (f0, f1, f2, f3)
    planes, rows, _, lanes = f0.shape
    height = rows * 8
    steps = planes // STEP
    first, last = slab[0] == 0, slab[0] == slabs - 1
    left, right = pencil[0] == 0, pencil[0] == pencils - 1
    row = lax.broadcasted_iota(jnp.int32, (8, lanes), 0)
    keep = jnp.where((right & (row < HALO)) | (left & (row >= HALO)), 0.0, 1.0)

    def send(i):
        here = pl.ds(i * STEP, STEP)
        copies = [pltpu.make_async_copy(potential_out.at[here], potential.at[here], sems.at[0])]
        for d in range(3):
            copies.append(pltpu.make_async_copy(gradient_out.at[d, here], gradient.at[d, here], sems.at[1 + d]))
        return copies

    def comb(t):
        return pl.ds(t, 8, stride=rows)

    def set_ends(x, value):
        for k, term in enumerate(z_terms(value)):
            ends[k, BASE + x] = term

    def set_y_faces(k):
        low, high = y_low[k], y_high[k]
        for half in range(2):
            set_ends(2 * k + half, y_ends(low, high, half) * keep)

    if inner:
        @pl.loop(0, planes // 16)
        def _(k):
            for j in range(8):
                set_y_faces(8 * k + j)
    else:
        for j in range(8):
            set_y_faces(j)
            set_y_faces(planes // 2 - 1 - j)
        (beyond,) = rest
        for i in range(HALO):
            for edge, x, face in ((first, i - HALO, x_low), (last, planes + i, x_high)):
                scale = jnp.where(edge, 0.0, 1.0)
                for t in range(rows):
                    for k, term in enumerate(z_terms(face[i, t] * scale)):
                        beyond[k, x % (2 * HALO), t] = term
                set_ends(x, face[i, rows] * (keep * scale))

    def given(k, x):
        if isinstance(x, int) and not 0 <= x < planes:
            return tuple(beyond[k, x % (2 * HALO), t] for t in range(rows)) + (ends[k, BASE + x],)
        return tuple(fields[k][x, t] for t in range(rows)) + (ends[k, BASE + x],)

    def load(field, x):
        return tuple(field[BASE + x, t] for t in range(rows + 1))

    def along_y(here):
        side = here[rows]
        below = (pltpu.roll(jnp.where(row == 7, side, here[rows - 1]), 1, 0),) + here[: rows - 1]
        above = here[1:rows] + (pltpu.roll(jnp.where(row == 0, side, here[0]), 7, 0),)
        below += (pltpu.roll(jnp.where(row == 7, here[rows - 1], side), 1, 0),)
        above += (pltpu.roll(jnp.where(row == 0, here[0], side), 7, 0),)
        return below, above

    def sweep(k, start, count, reads=None):
        old, new = ((None, v1), (v1, v2), (v2, v3))[k]
        read = functools.partial(given, 0) if k == 0 else functools.partial(load, old)
        reads = start if k == 0 or reads is None else reads
        before, here = read(reads - 1), read(reads)
        for j in range(count):
            x = start + j
            after = read(reads + j + 1)
            term = given(k + 1, x)
            below, above = along_y(here)
            for t in range(rows + 1):
                around = (before[t] + after[t]) + (below[t] + above[t]) + 3.0 * here[t]
                value = term[t] + around * (1.0 / 9.0)
                value = value * keep if t == rows else value
                new[BASE + x, t] = value
            before, here = here, after

    def clear(field, start):
        for i in range(HALO):
            field[BASE + start + i] = jnp.zeros((rows + 1, 8, lanes), F32)

    def begin(i):
        for k, field in enumerate((v1, v2, v3)):
            sweep(k, i * STEP - 3 + k, 6 - 2 * k)
            if not inner and i == 0:
                pl.when(first)(functools.partial(clear, field, -HALO))

    def advance(i, at=None):
        at = i * STEP if at is None else at
        for k, field in enumerate((v1, v2, v3)):
            sweep(k, i * STEP + 3 - k, STEP, at + 3 - k)
            if not inner and i == steps - 1:
                pl.when(last)(functools.partial(clear, field, planes))
        x0 = i * STEP
        before, here = load(v3, at - 1), load(v3, at)
        for j in range(STEP):
            x = x0 + j
            after = load(v3, at + j + 1)
            below, above = along_y(here)
            for t in range(rows):
                down, up = along_z(here[t])
                potential_out[x, comb(t), :] = here[t] * (1.0 / 9.0)
                gradient_out[0, x, comb(t), :] = (after[t] - before[t]) * (0.5 / 9.0)
                gradient_out[1, x, comb(t), :] = (above[t] - below[t]) * (0.5 / 9.0)
                gradient_out[2, x, comb(t), :] = (up - down) * (0.5 / 9.0)
            before, here = here, after
        for copy in send(i):
            copy.start()
        return at + STEP

    if inner:
        begin(1)
        lax.fori_loop(1, steps - 1, advance, jnp.maximum(slab[0] - slabs, STEP))

        @pl.loop(1, steps - 1)
        def _(i):
            for copy in send(i):
                copy.wait()
    else:
        for i in (0, steps - 1):
            begin(i)
            advance(i)
        for i in (0, steps - 1):
            for copy in send(i):
                copy.wait()


def sweeps(inner, place, fields, y_faces, x_faces, results, slabs, pencils):
    planes, rows, _, lanes = fields[0].shape
    height = rows * 8
    ends = pltpu.VMEM((4, BASE + planes + BASE, 8, lanes), F32)
    field = pltpu.VMEM((BASE + planes + BASE, rows + 1, 8, lanes), F32)
    vmem, hbm = pl.BlockSpec(memory_space=pltpu.VMEM), pl.BlockSpec(memory_space=pl.ANY)
    scratch = [
        ends, field, field, field,
        pltpu.VMEM((planes, height, lanes), F32),
        pltpu.VMEM((3, planes, height, lanes), F32),
        pltpu.SemaphoreType.DMA((4,)),
    ]
    if not inner:
        scratch.append(pltpu.VMEM((4, 2 * HALO, rows, 8, lanes), F32))
    return pl.pallas_call(
        functools.partial(sweep_kernel, inner, slabs, pencils),
        out_shape=[
            jax.ShapeDtypeStruct((planes, height, lanes), F32),
            jax.ShapeDtypeStruct((3, planes, height, lanes), F32),
        ],
        in_specs=[pl.BlockSpec(memory_space=pltpu.SMEM)] * 2 + [vmem] * (6 + len(x_faces)) + [hbm] * len(results),
        out_specs=[hbm, hbm],
        scratch_shapes=scratch,
        input_output_aliases={} if inner else {10: 0, 11: 1},
        compiler_params=pltpu.CompilerParams(vmem_limit_bytes=28 << 20),
        cost_estimate=pl.CostEstimate(flops=1 << 25, bytes_accessed=(24 if inner else 4) << 20, transcendentals=0),
        name="inner_sweeps" if inner else "edge_sweeps",
    )(*place, *fields, *y_faces, *x_faces, *results)


def ring(values, axis, count):
    up = [(i, (i + 1) % count) for i in range(count)]
    down = [((i + 1) % count, i) for i in range(count)]
    low, high = values
    return lax.ppermute(high, axis, up), lax.ppermute(low, axis, down)


def on_device(fine, coarse, anchor, extent, owner, count):
    slabs, pencils = lax.axis_size("slab"), lax.axis_size("pencil")
    place = [lax.axis_index(name).astype(jnp.int32).reshape(1) for name in ("slab", "pencil")]
    sent = average(place, fine, anchor, extent, owner, count, slabs)
    received = lax.all_to_all(sent, "slab", split_axis=0, concat_axis=0, tiled=True)
    source, y_low, y_high = deposit(received, coarse)
    fields = prepare(source)
    y_low, y_high = ring((y_low, y_high), "pencil", pencils)

    x_low, x_high = ring(faces(fields[0], y_low, y_high), "slab", slabs)
    y_faces = (y_low, y_high)
    results = sweeps(True, place, fields, y_faces, (), (), slabs, pencils)
    potential, gradient = sweeps(False, place, fields, y_faces, (x_low, x_high), results, slabs, pencils)
    return potential, gradient


def solution(mesh):
    in_specs = (
        P("slab", "pencil", None, None, None, None),
        P("slab", "pencil", None),
        P("slab", "pencil", None, None),
        P("slab", "pencil", None, None),
        P("slab", "pencil", None, None),
        P("slab", "pencil"),
    )
    out_specs = (P("slab", "pencil", None), P(None, "slab", "pencil", None))
    return jax.shard_map(
        on_device, mesh=mesh, in_specs=in_specs, out_specs=out_specs, check_vma=False
    )
```

```python
import functools

import jax
import jax.numpy as jnp
from jax import lax
from jax.experimental import pallas as pl
from jax.experimental.pallas import tpu as pltpu
from jax.sharding import PartitionSpec as P

HALO = 4
META_ROWS = 8
STEP = 8
BASE = 8
GROUP = 16
DEEP = 4
F32 = jnp.float32


def average_kernel(slab, pencil, anchor, extent, owners, count, fine, sent, cells, packed, blank, in_sems, out_sem, blank_sem):
    slots, fine_edge = cells.shape[:2]
    rows = packed.shape[1] - META_ROWS
    edge = fine_edge // 2
    lanes = packed.shape[2]
    groups = lanes // edge
    tiles = edge // groups
    parts = in_sems.shape[1]
    share = fine_edge // parts

    def load(p, part):
        here = pl.ds(part * share, share)
        return pltpu.make_async_copy(fine.at[0, 0, p, here], cells.at[p, here], in_sems.at[p, part])

    def store(p):
        return pltpu.make_async_copy(packed.at[p], sent.at[owners[0, 0, 0, p]], out_sem)

    def clear():
        return pltpu.make_async_copy(blank, sent.at[:, pl.ds(rows, META_ROWS), :], blank_sem)

    for p in range(slots):
        for part in range(parts):
            load(p, part).start()
    blank[...] = jnp.zeros_like(blank)
    clear().start()
    lane = lax.broadcasted_iota(jnp.int32, (META_ROWS, lanes), 1)
    source_lane = lax.broadcasted_iota(jnp.int32, (fine_edge, lanes), 0)
    target_lane = lax.broadcasted_iota(jnp.int32, (fine_edge, lanes), 1)

    @pl.loop(0, slots)
    def _(p):
        for part in range(parts):
            load(p, part).wait()
        total = jnp.zeros((rows, lanes), F32)
        for g in range(groups):
            pieces = [
                cells[p, pl.ds(2 * g + dx, tiles, stride=2 * groups), pl.ds(dy, edge, stride=2), :]
                for dx in range(2) for dy in range(2)
            ]
            part = ((pieces[0] + pieces[1]) + (pieces[2] + pieces[3])).reshape(rows, fine_edge)
            high = part.astype(jnp.bfloat16)
            low = (part - high.astype(F32)).astype(jnp.bfloat16)
            gather = jnp.where(target_lane == g * edge + source_lane // 2, 0.125, 0.0).astype(jnp.bfloat16)
            total = total + jnp.dot(high, gather, preferred_element_type=F32)
            total = total + jnp.dot(low, gather, preferred_element_type=F32)
        packed[p, :rows, :] = total
        alive = (p < count[0, 0]).astype(jnp.int32)
        words = jnp.where(lane == 0, alive, 0)
        for d in range(3):
            words = jnp.where(lane == 1 + d, anchor[0, d, 0, p], words)
            words = jnp.where(lane == 4 + d, lax.shift_right_logical(extent[0, d, 0, p], 1), words)
        packed[p, pl.ds(rows, META_ROWS), :] = words.astype(F32)
        pl.when(p == 0)(lambda: clear().wait())
        store(p).start()

    @pl.loop(0, slots)
    def _(p):
        store(p).wait()


def average(place, fine, anchor, extent, owner, count, slabs):
    by_component = lambda a: jnp.transpose(a, (0, 3, 1, 2))
    slots, fine_edge = fine.shape[2], fine.shape[3]
    edge = fine_edge // 2
    rows = edge * edge * edge // 128
    smem = pl.BlockSpec(memory_space=pltpu.SMEM)
    return pl.pallas_call(
        average_kernel,
        out_shape=jax.ShapeDtypeStruct((slabs, rows + META_ROWS, 128), F32),
        in_specs=[smem] * 6 + [pl.BlockSpec(memory_space=pl.ANY)],
        out_specs=pl.BlockSpec(memory_space=pl.ANY),
        scratch_shapes=[
            pltpu.VMEM(fine.shape[2:], F32),
            pltpu.VMEM((slots, rows + META_ROWS, 128), F32),
            pltpu.VMEM((slabs, META_ROWS, 128), F32),
            pltpu.SemaphoreType.DMA((slots, 2)),
            pltpu.SemaphoreType.DMA,
            pltpu.SemaphoreType.DMA,
        ],
        compiler_params=pltpu.CompilerParams(vmem_limit_bytes=56 << 20),
        name="average",
    )(*place, by_component(anchor), by_component(extent), by_component(owner), count, fine)


def deposit_kernel(received, coarse, source, y_low, y_high, words, sem):
    slabs, all_rows, lanes = received.shape
    rows = all_rows - META_ROWS
    edge = 32
    groups = lanes // edge
    planes, height, _ = source.shape
    for s in range(slabs):
        pltpu.make_async_copy(received.at[s, rows], words.at[s], sem).start()
    source[...] = jnp.zeros_like(source)
    for s in range(slabs):
        pltpu.make_async_copy(received.at[s, rows], words.at[s], sem).wait()
    row = lax.broadcasted_iota(jnp.int32, (edge, lanes), 0)
    lane = lax.broadcasted_iota(jnp.int32, (edge, lanes), 1)

    @pl.loop(0, slabs)
    def _(s):
        word = lambda k: words[s, k].astype(jnp.int32)

        @pl.when(word(0) > 0)
        def _():
            ax, ay, az, hx, hy, hz = (word(k) for k in range(1, 7))
            covered = (row < hy) & (lane >= az) & (lane < az + hz)
            here = pl.ds(ay, edge)

            @pl.loop(0, lax.div(hx + DEEP * groups - 1, DEEP * groups))
            def _(part):
                results = []
                for n in range(DEEP):
                    tile = part * DEEP + n
                    data = received[s, pl.ds(pl.multiple_of(tile * edge, edge), edge), :]
                    for g in range(groups):
                        i = tile * groups + g
                        x = ax + i
                        moved = pltpu.roll(data, lax.rem(az + lanes - g * edge, lanes), 1)
                        change = jnp.where(covered & (i < hx), moved - coarse[x, here, :], 0.0)
                        results.append((x, source[x, here, :] + change))
                for x, value in results:
                    source[x, here, :] = value

    row8 = lax.broadcasted_iota(jnp.int32, (2 * HALO, lanes), 0)

    @pl.loop(0, planes // 16)
    def _(part):
        for j in range(8):
            k = part * 8 + j
            for face, start, split in ((y_low, 0, HALO), (y_high, height - 2 * HALO, 0)):
                one, two = source[2 * k, start : start + 8, :], source[2 * k + 1, start : start + 8, :]
                if split:
                    face[k] = jnp.where(row8 < HALO, one, pltpu.roll(two, HALO, 0))
                else:
                    face[k] = jnp.where(row8 < HALO, pltpu.roll(one, HALO, 0), two)


def deposit(received, coarse):
    planes, height, lanes = coarse.shape
    face = jax.ShapeDtypeStruct((planes // 2, 2 * HALO, lanes), F32)
    vmem = pl.BlockSpec(memory_space=pltpu.VMEM)
    return pl.pallas_call(
        deposit_kernel,
        out_shape=[jax.ShapeDtypeStruct(coarse.shape, F32), face, face],
        in_specs=[vmem, vmem],
        out_specs=[vmem, vmem, vmem],
        scratch_shapes=[pltpu.SMEM((received.shape[0], lanes), F32), pltpu.SemaphoreType.DMA],
        compiler_params=pltpu.CompilerParams(vmem_limit_bytes=12 << 20),
        name="deposit",
    )(received, coarse)


def along_z(value):
    lanes = value.shape[1]
    lane = lax.broadcasted_iota(jnp.int32, value.shape, 1)
    down = jnp.where(lane == 0, 0.0, pltpu.roll(value, 1, 1))
    up = jnp.where(lane == lanes - 1, 0.0, pltpu.roll(value, lanes - 1, 1))
    return down, up


def z_terms(value):
    lanes = value.shape[1]
    lane = lax.broadcasted_iota(jnp.int32, value.shape, 1)
    down = [None] + [jnp.where(lane < d, 0.0, pltpu.roll(value, d, 1)) for d in (1, 2, 3)]
    up = [None] + [jnp.where(lane >= lanes - d, 0.0, pltpu.roll(value, lanes - d, 1)) for d in (1, 2, 3)]
    outer = (lane == 0) | (lane == lanes - 1)
    once = down[1] + up[1]
    twice = (down[2] + up[2]) + jnp.where(outer, 1.0, 2.0) * value
    thrice = (down[3] + up[3]) + (
        jnp.where((lane == 0) | (lane == lanes - 2), 2.0, 3.0) * up[1]
        + jnp.where((lane == 1) | (lane == lanes - 1), 2.0, 3.0) * down[1]
    )
    return (
        value,
        value + once * (1.0 / 3.0),
        value + (once * (2.0 / 9.0) + twice * (1.0 / 27.0)),
        (value + once * (1.0 / 9.0)) + (twice * (1.0 / 81.0) + thrice * (1.0 / 729.0)),
    )


def prepare_kernel(source, *fields):
    planes, height, _ = source.shape
    rows = height // 8

    @pl.loop(0, planes // GROUP)
    def _(k):
        for j in range(GROUP):
            for t in range(rows):
                for field, term in zip(fields, z_terms(source[GROUP * k + j, pl.ds(t, 8, stride=rows), :])):
                    field[GROUP * k + j, t] = term


def prepare(source):
    planes, height, lanes = source.shape
    field = jax.ShapeDtypeStruct((planes, height // 8, 8, lanes), F32)
    vmem = pl.BlockSpec(memory_space=pltpu.VMEM)
    return pl.pallas_call(
        prepare_kernel,
        out_shape=[field] * 4,
        in_specs=[vmem],
        out_specs=[vmem] * 4,
        compiler_params=pltpu.CompilerParams(vmem_limit_bytes=20 << 20),
        cost_estimate=pl.CostEstimate(flops=1 << 25, bytes_accessed=15 << 20, transcendentals=0),
        name="prepare",
    )(source)


def y_ends(low, high, half):
    row = lax.broadcasted_iota(jnp.int32, low.shape, 0)
    if half == 0:
        return jnp.where(row < HALO, high, pltpu.roll(low, HALO, 0))
    return jnp.where(row < HALO, pltpu.roll(high, HALO, 0), low)


def faces_kernel(field, y_low, y_high, x_low, x_high):
    planes, rows, _, _ = field.shape
    for face, start in ((x_low, 0), (x_high, planes - HALO)):
        for i in range(HALO):
            k, half = divmod(start + i, 2)
            for t in range(rows):
                face[i, t] = field[start + i, t]
            face[i, rows] = y_ends(y_low[k], y_high[k], half)


def faces(field, y_low, y_high):
    face = jax.ShapeDtypeStruct((HALO, field.shape[1] + 1) + field.shape[2:], F32)
    vmem = pl.BlockSpec(memory_space=pltpu.VMEM)
    return pl.pallas_call(
        faces_kernel,
        out_shape=[face, face],
        in_specs=[vmem] * 3,
        out_specs=[vmem] * 2,
        compiler_params=pltpu.CompilerParams(vmem_limit_bytes=4 << 20),
        name="faces",
    )(field, y_low, y_high)


def sweep_kernel(inner, slabs, pencils, slab, pencil, f0, f1, f2, f3, y_low, y_high, *rest):
    if inner:
        potential, gradient, *rest = rest
    else:
        x_low, x_high, _, _, potential, gradient, *rest = rest
    ends, v1, v2, v3, potential_out, gradient_out, sems, *rest = rest
    fields = (f0, f1, f2, f3)
    planes, rows, _, lanes = f0.shape
    height = rows * 8
    steps = planes // STEP
    first, last = slab[0] == 0, slab[0] == slabs - 1
    left, right = pencil[0] == 0, pencil[0] == pencils - 1
    row = lax.broadcasted_iota(jnp.int32, (8, lanes), 0)
    keep = jnp.where((right & (row < HALO)) | (left & (row >= HALO)), 0.0, 1.0)

    def send(i):
        here = pl.ds(i * STEP, STEP)
        copies = [pltpu.make_async_copy(potential_out.at[here], potential.at[here], sems.at[0])]
        for d in range(3):
            copies.append(pltpu.make_async_copy(gradient_out.at[d, here], gradient.at[d, here], sems.at[1 + d]))
        return copies

    def comb(t):
        return pl.ds(t, 8, stride=rows)

    def set_ends(x, value):
        for k, term in enumerate(z_terms(value)):
            ends[k, BASE + x] = term

    def set_y_faces(k):
        low, high = y_low[k], y_high[k]
        for half in range(2):
            set_ends(2 * k + half, y_ends(low, high, half) * keep)

    if inner:
        @pl.loop(0, planes // 16)
        def _(k):
            for j in range(8):
                set_y_faces(8 * k + j)
    else:
        for j in range(8):
            set_y_faces(j)
            set_y_faces(planes // 2 - 1 - j)
        (beyond,) = rest
        for i in range(HALO):
            for edge, x, face in ((first, i - HALO, x_low), (last, planes + i, x_high)):
                scale = jnp.where(edge, 0.0, 1.0)
                for t in range(rows):
                    for k, term in enumerate(z_terms(face[i, t] * scale)):
                        beyond[k, x % (2 * HALO), t] = term
                set_ends(x, face[i, rows] * (keep * scale))

    def given(k, x):
        if isinstance(x, int) and not 0 <= x < planes:
            return tuple(beyond[k, x % (2 * HALO), t] for t in range(rows)) + (ends[k, BASE + x],)
        return tuple(fields[k][x, t] for t in range(rows)) + (ends[k, BASE + x],)

    def load(field, x):
        return tuple(field[BASE + x, t] for t in range(rows + 1))

    def along_y(here):
        side = here[rows]
        below = (pltpu.roll(jnp.where(row == 7, side, here[rows - 1]), 1, 0),) + here[: rows - 1]
        above = here[1:rows] + (pltpu.roll(jnp.where(row == 0, side, here[0]), 7, 0),)
        below += (pltpu.roll(jnp.where(row == 7, here[rows - 1], side), 1, 0),)
        above += (pltpu.roll(jnp.where(row == 0, here[0], side), 7, 0),)
        return below, above

    def sweep(k, start, count, reads=None):
        old, new = ((None, v1), (v1, v2), (v2, v3))[k]
        read = functools.partial(given, 0) if k == 0 else functools.partial(load, old)
        reads = start if k == 0 or reads is None else reads
        before, here = read(reads - 1), read(reads)
        for j in range(count):
            x = start + j
            after = read(reads + j + 1)
            term = given(k + 1, x)
            below, above = along_y(here)
            for t in range(rows + 1):
                around = (before[t] + after[t]) + (below[t] + above[t]) + 3.0 * here[t]
                value = term[t] + around * (1.0 / 9.0)
                value = value * keep if t == rows else value
                new[BASE + x, t] = value
            before, here = here, after

    def clear(field, start):
        for i in range(HALO):
            field[BASE + start + i] = jnp.zeros((rows + 1, 8, lanes), F32)

    def begin(i):
        for k, field in enumerate((v1, v2, v3)):
            sweep(k, i * STEP - 3 + k, 6 - 2 * k)
            if not inner and i == 0:
                pl.when(first)(functools.partial(clear, field, -HALO))

    def advance(i, at=None):
        at = i * STEP if at is None else at
        for k, field in enumerate((v1, v2, v3)):
            sweep(k, i * STEP + 3 - k, STEP, at + 3 - k)
            if not inner and i == steps - 1:
                pl.when(last)(functools.partial(clear, field, planes))
        x0 = i * STEP
        before, here = load(v3, at - 1), load(v3, at)
        for j in range(STEP):
            x = x0 + j
            after = load(v3, at + j + 1)
            below, above = along_y(here)
            for t in range(rows):
                down, up = along_z(here[t])
                potential_out[x, comb(t), :] = here[t] * (1.0 / 9.0)
                gradient_out[0, x, comb(t), :] = (after[t] - before[t]) * (0.5 / 9.0)
                gradient_out[1, x, comb(t), :] = (above[t] - below[t]) * (0.5 / 9.0)
                gradient_out[2, x, comb(t), :] = (up - down) * (0.5 / 9.0)
            before, here = here, after
        for copy in send(i):
            copy.start()
        return at + STEP

    if inner:
        begin(1)
        lax.fori_loop(1, steps - 1, advance, jnp.maximum(slab[0] - slabs, STEP))

        @pl.loop(1, steps - 1)
        def _(i):
            for copy in send(i):
                copy.wait()
    else:
        for i in (0, steps - 1):
            begin(i)
            advance(i)
        for i in (0, steps - 1):
            for copy in send(i):
                copy.wait()


def sweeps(inner, place, fields, y_faces, x_faces, results, slabs, pencils):
    planes, rows, _, lanes = fields[0].shape
    height = rows * 8
    ends = pltpu.VMEM((4, BASE + planes + BASE, 8, lanes), F32)
    field = pltpu.VMEM((BASE + planes + BASE, rows + 1, 8, lanes), F32)
    vmem, hbm = pl.BlockSpec(memory_space=pltpu.VMEM), pl.BlockSpec(memory_space=pl.ANY)
    scratch = [
        ends, field, field, field,
        pltpu.VMEM((planes, height, lanes), F32),
        pltpu.VMEM((3, planes, height, lanes), F32),
        pltpu.SemaphoreType.DMA((4,)),
    ]
    if not inner:
        scratch.append(pltpu.VMEM((4, 2 * HALO, rows, 8, lanes), F32))
    return pl.pallas_call(
        functools.partial(sweep_kernel, inner, slabs, pencils),
        out_shape=[
            jax.ShapeDtypeStruct((planes, height, lanes), F32),
            jax.ShapeDtypeStruct((3, planes, height, lanes), F32),
        ],
        in_specs=[pl.BlockSpec(memory_space=pltpu.SMEM)] * 2 + [vmem] * (6 + len(x_faces)) + [hbm] * len(results),
        out_specs=[hbm, hbm],
        scratch_shapes=scratch,
        input_output_aliases={} if inner else {10: 0, 11: 1},
        compiler_params=pltpu.CompilerParams(vmem_limit_bytes=28 << 20),
        cost_estimate=pl.CostEstimate(flops=1 << 25, bytes_accessed=(24 if inner else 4) << 20, transcendentals=0),
        name="inner_sweeps" if inner else "edge_sweeps",
    )(*place, *fields, *y_faces, *x_faces, *results)


def ring(values, axis, count):
    up = [(i, (i + 1) % count) for i in range(count)]
    down = [((i + 1) % count, i) for i in range(count)]
    low, high = values
    return lax.ppermute(high, axis, up), lax.ppermute(low, axis, down)


def on_device(fine, coarse, anchor, extent, owner, count):
    slabs, pencils = lax.axis_size("slab"), lax.axis_size("pencil")
    place = [lax.axis_index(name).astype(jnp.int32).reshape(1) for name in ("slab", "pencil")]
    sent = average(place, fine, anchor, extent, owner, count, slabs)
    received = lax.all_to_all(sent, "slab", split_axis=0, concat_axis=0, tiled=True)
    source, y_low, y_high = deposit(received, coarse)
    fields = prepare(source)
    y_low, y_high = ring((y_low, y_high), "pencil", pencils)

    x_low, x_high = ring(faces(fields[0], y_low, y_high), "slab", slabs)
    y_faces = (y_low, y_high)
    results = sweeps(True, place, fields, y_faces, (), (), slabs, pencils)
    potential, gradient = sweeps(False, place, fields, y_faces, (x_low, x_high), results, slabs, pencils)
    return potential, gradient


def solution(mesh):
    in_specs = (
        P("slab", "pencil", None, None, None, None),
        P("slab", "pencil", None),
        P("slab", "pencil", None, None),
        P("slab", "pencil", None, None),
        P("slab", "pencil", None, None),
        P("slab", "pencil"),
    )
    out_specs = (P("slab", "pencil", None), P(None, "slab", "pencil", None))
    return jax.shard_map(
        on_device, mesh=mesh, in_specs=in_specs, out_specs=out_specs, check_vma=False
    )
```

```python
import functools

import jax
import jax.numpy as jnp
from jax import lax
from jax.experimental import pallas as pl
from jax.experimental.pallas import tpu as pltpu
from jax.sharding import PartitionSpec as P

HALO = 4
META_ROWS = 8
STEP = 8
BASE = 8
GROUP = 16
DEEP = 4
F32 = jnp.float32


def average_kernel(slab, pencil, anchor, extent, owners, count, fine, sent, cells, sems):
    slots, fine_edge = cells.shape[:2]
    rows = sent.shape[1] - META_ROWS
    edge = fine_edge // 2
    lanes = sent.shape[2]
    groups = lanes // edge
    tiles = edge // groups
    share = 2 * groups

    def each_part(p, act):
        planes, lines = extent[0, 0, 0, p], extent[0, 1, 0, p]

        @pl.loop(0, jnp.minimum(lax.div(planes + share - 1, share), tiles))
        def _(tile):
            here = pl.ds(pl.multiple_of(tile * share, share), share)

            def part(half):
                there = pl.ds(half * edge, edge)
                return pltpu.make_async_copy(fine.at[0, 0, p, here, there], cells.at[p, here, there], sems.at[p])

            act(part(0))
            pl.when(lines > edge)(lambda: act(part(1)))

    live = jnp.minimum(count[0, 0], slots)

    @pl.loop(0, live)
    def _(p):
        each_part(p, lambda copy: copy.start())

    lane = lax.broadcasted_iota(jnp.int32, (META_ROWS, lanes), 1)
    source_lane = lax.broadcasted_iota(jnp.int32, (fine_edge, lanes), 0)
    target_lane = lax.broadcasted_iota(jnp.int32, (fine_edge, lanes), 1)
    for slot in range(sent.shape[0]):
        sent[slot, pl.ds(rows, META_ROWS), :] = jnp.zeros((META_ROWS, lanes), F32)

    @pl.loop(0, live)
    def _(p):
        each_part(p, lambda copy: copy.wait())
        owner = owners[0, 0, 0, p]
        total = jnp.zeros((rows, lanes), F32)
        for g in range(groups):
            pieces = [
                cells[p, pl.ds(2 * g + dx, tiles, stride=2 * groups), pl.ds(dy, edge, stride=2), :]
                for dx in range(2) for dy in range(2)
            ]
            part = ((pieces[0] + pieces[1]) + (pieces[2] + pieces[3])).reshape(rows, fine_edge)
            high = part.astype(jnp.bfloat16)
            low = (part - high.astype(F32)).astype(jnp.bfloat16)
            gather = jnp.where(target_lane == g * edge + source_lane // 2, 0.125, 0.0).astype(jnp.bfloat16)
            total = total + jnp.dot(high, gather, preferred_element_type=F32)
            total = total + jnp.dot(low, gather, preferred_element_type=F32)
        sent[owner, :rows, :] = total
        words = jnp.where(lane == 0, 1, 0)
        for d in range(3):
            words = jnp.where(lane == 1 + d, anchor[0, d, 0, p], words)
            words = jnp.where(lane == 4 + d, lax.shift_right_logical(extent[0, d, 0, p], 1), words)
        sent[owner, pl.ds(rows, META_ROWS), :] = words.astype(F32)


def average(place, fine, anchor, extent, owner, count, slabs):
    by_component = lambda a: jnp.transpose(a, (0, 3, 1, 2))
    slots, fine_edge = fine.shape[2], fine.shape[3]
    edge = fine_edge // 2
    rows = edge * edge * edge // 128
    smem = pl.BlockSpec(memory_space=pltpu.SMEM)
    return pl.pallas_call(
        average_kernel,
        out_shape=jax.ShapeDtypeStruct((slabs, rows + META_ROWS, 128), F32),
        in_specs=[smem] * 6 + [pl.BlockSpec(memory_space=pl.ANY)],
        out_specs=pl.BlockSpec(memory_space=pltpu.VMEM),
        scratch_shapes=[pltpu.VMEM(fine.shape[2:], F32), pltpu.SemaphoreType.DMA((slots,))],
        compiler_params=pltpu.CompilerParams(vmem_limit_bytes=56 << 20),
        name="average",
    )(*place, by_component(anchor), by_component(extent), by_component(owner), count, fine)


def deposit_kernel(received, coarse, source, y_low, y_high, words, sem):
    slabs, all_rows, lanes = received.shape
    rows = all_rows - META_ROWS
    edge = 32
    groups = lanes // edge
    planes, height, _ = source.shape
    for s in range(slabs):
        pltpu.make_async_copy(received.at[s, rows], words.at[s], sem).start()
    source[...] = jnp.zeros_like(source)
    for s in range(slabs):
        pltpu.make_async_copy(received.at[s, rows], words.at[s], sem).wait()
    row = lax.broadcasted_iota(jnp.int32, (edge, lanes), 0)
    lane = lax.broadcasted_iota(jnp.int32, (edge, lanes), 1)

    @pl.loop(0, slabs)
    def _(s):
        word = lambda k: words[s, k].astype(jnp.int32)

        @pl.when(word(0) > 0)
        def _():
            ax, ay, az, hx, hy, hz = (word(k) for k in range(1, 7))
            covered = (row < hy) & (lane >= az) & (lane < az + hz)
            here = pl.ds(ay, edge)

            @pl.loop(0, lax.div(hx + DEEP * groups - 1, DEEP * groups))
            def _(part):
                results = []
                for n in range(DEEP):
                    tile = part * DEEP + n
                    data = received[s, pl.ds(pl.multiple_of(tile * edge, edge), edge), :]
                    for g in range(groups):
                        i = tile * groups + g
                        x = ax + i
                        moved = pltpu.roll(data, lax.rem(az + lanes - g * edge, lanes), 1)
                        change = jnp.where(covered & (i < hx), moved - coarse[x, here, :], 0.0)
                        results.append((x, source[x, here, :] + change))
                for x, value in results:
                    source[x, here, :] = value

    row8 = lax.broadcasted_iota(jnp.int32, (2 * HALO, lanes), 0)

    @pl.loop(0, planes // 16)
    def _(part):
        for j in range(8):
            k = part * 8 + j
            for face, start, split in ((y_low, 0, HALO), (y_high, height - 2 * HALO, 0)):
                one, two = source[2 * k, start : start + 8, :], source[2 * k + 1, start : start + 8, :]
                if split:
                    face[k] = jnp.where(row8 < HALO, one, pltpu.roll(two, HALO, 0))
                else:
                    face[k] = jnp.where(row8 < HALO, pltpu.roll(one, HALO, 0), two)


def deposit(received, coarse):
    planes, height, lanes = coarse.shape
    face = jax.ShapeDtypeStruct((planes // 2, 2 * HALO, lanes), F32)
    vmem = pl.BlockSpec(memory_space=pltpu.VMEM)
    return pl.pallas_call(
        deposit_kernel,
        out_shape=[jax.ShapeDtypeStruct(coarse.shape, F32), face, face],
        in_specs=[vmem, vmem],
        out_specs=[vmem, vmem, vmem],
        scratch_shapes=[pltpu.SMEM((received.shape[0], lanes), F32), pltpu.SemaphoreType.DMA],
        compiler_params=pltpu.CompilerParams(vmem_limit_bytes=12 << 20),
        name="deposit",
    )(received, coarse)


def along_z(value):
    lanes = value.shape[1]
    lane = lax.broadcasted_iota(jnp.int32, value.shape, 1)
    down = jnp.where(lane == 0, 0.0, pltpu.roll(value, 1, 1))
    up = jnp.where(lane == lanes - 1, 0.0, pltpu.roll(value, lanes - 1, 1))
    return down, up


def z_terms(value):
    lanes = value.shape[1]
    lane = lax.broadcasted_iota(jnp.int32, value.shape, 1)
    down = [None] + [jnp.where(lane < d, 0.0, pltpu.roll(value, d, 1)) for d in (1, 2, 3)]
    up = [None] + [jnp.where(lane >= lanes - d, 0.0, pltpu.roll(value, lanes - d, 1)) for d in (1, 2, 3)]
    outer = (lane == 0) | (lane == lanes - 1)
    once = down[1] + up[1]
    twice = (down[2] + up[2]) + jnp.where(outer, 1.0, 2.0) * value
    thrice = (down[3] + up[3]) + (
        jnp.where((lane == 0) | (lane == lanes - 2), 2.0, 3.0) * up[1]
        + jnp.where((lane == 1) | (lane == lanes - 1), 2.0, 3.0) * down[1]
    )
    return (
        value,
        value + once * (1.0 / 3.0),
        value + (once * (2.0 / 9.0) + twice * (1.0 / 27.0)),
        (value + once * (1.0 / 9.0)) + (twice * (1.0 / 81.0) + thrice * (1.0 / 729.0)),
    )


def prepare_kernel(source, *fields):
    planes, height, _ = source.shape
    rows = height // 8

    @pl.loop(0, planes // GROUP)
    def _(k):
        for j in range(GROUP):
            for t in range(rows):
                for field, term in zip(fields, z_terms(source[GROUP * k + j, pl.ds(t, 8, stride=rows), :])):
                    field[GROUP * k + j, t] = term


def prepare(source):
    planes, height, lanes = source.shape
    field = jax.ShapeDtypeStruct((planes, height // 8, 8, lanes), F32)
    vmem = pl.BlockSpec(memory_space=pltpu.VMEM)
    return pl.pallas_call(
        prepare_kernel,
        out_shape=[field] * 4,
        in_specs=[vmem],
        out_specs=[vmem] * 4,
        compiler_params=pltpu.CompilerParams(vmem_limit_bytes=20 << 20),
        cost_estimate=pl.CostEstimate(flops=1 << 25, bytes_accessed=15 << 20, transcendentals=0),
        name="prepare",
    )(source)


def y_ends(low, high, half):
    row = lax.broadcasted_iota(jnp.int32, low.shape, 0)
    if half == 0:
        return jnp.where(row < HALO, high, pltpu.roll(low, HALO, 0))
    return jnp.where(row < HALO, pltpu.roll(high, HALO, 0), low)


def faces_kernel(field, y_low, y_high, x_low, x_high):
    planes, rows, _, _ = field.shape
    for face, start in ((x_low, 0), (x_high, planes - HALO)):
        for i in range(HALO):
            k, half = divmod(start + i, 2)
            for t in range(rows):
                face[i, t] = field[start + i, t]
            face[i, rows] = y_ends(y_low[k], y_high[k], half)


def faces(field, y_low, y_high):
    face = jax.ShapeDtypeStruct((HALO, field.shape[1] + 1) + field.shape[2:], F32)
    vmem = pl.BlockSpec(memory_space=pltpu.VMEM)
    return pl.pallas_call(
        faces_kernel,
        out_shape=[face, face],
        in_specs=[vmem] * 3,
        out_specs=[vmem] * 2,
        compiler_params=pltpu.CompilerParams(vmem_limit_bytes=4 << 20),
        name="faces",
    )(field, y_low, y_high)


def sweep_kernel(inner, slabs, pencils, slab, pencil, f0, f1, f2, f3, y_low, y_high, *rest):
    if inner:
        potential, gradient, *rest = rest
    else:
        x_low, x_high, _, _, potential, gradient, *rest = rest
    ends, v1, v2, v3, potential_out, gradient_out, sems, *rest = rest
    fields = (f0, f1, f2, f3)
    planes, rows, _, lanes = f0.shape
    height = rows * 8
    steps = planes // STEP
    first, last = slab[0] == 0, slab[0] == slabs - 1
    left, right = pencil[0] == 0, pencil[0] == pencils - 1
    row = lax.broadcasted_iota(jnp.int32, (8, lanes), 0)
    keep = jnp.where((right & (row < HALO)) | (left & (row >= HALO)), 0.0, 1.0)

    def send(i):
        here = pl.ds(i * STEP, STEP)
        copies = [pltpu.make_async_copy(potential_out.at[here], potential.at[here], sems.at[0])]
        for d in range(3):
            copies.append(pltpu.make_async_copy(gradient_out.at[d, here], gradient.at[d, here], sems.at[1 + d]))
        return copies

    def comb(t):
        return pl.ds(t, 8, stride=rows)

    def set_ends(x, value):
        for k, term in enumerate(z_terms(value)):
            ends[k, BASE + x] = term

    def set_y_faces(k):
        low, high = y_low[k], y_high[k]
        for half in range(2):
            set_ends(2 * k + half, y_ends(low, high, half) * keep)

    if inner:
        @pl.loop(0, planes // 16)
        def _(k):
            for j in range(8):
                set_y_faces(8 * k + j)
    else:
        for j in range(8):
            set_y_faces(j)
            set_y_faces(planes // 2 - 1 - j)
        (beyond,) = rest
        for i in range(HALO):
            for edge, x, face in ((first, i - HALO, x_low), (last, planes + i, x_high)):
                scale = jnp.where(edge, 0.0, 1.0)
                for t in range(rows):
                    for k, term in enumerate(z_terms(face[i, t] * scale)):
                        beyond[k, x % (2 * HALO), t] = term
                set_ends(x, face[i, rows] * (keep * scale))

    def given(k, x):
        if isinstance(x, int) and not 0 <= x < planes:
            return tuple(beyond[k, x % (2 * HALO), t] for t in range(rows)) + (ends[k, BASE + x],)
        return tuple(fields[k][x, t] for t in range(rows)) + (ends[k, BASE + x],)

    def load(field, x):
        return tuple(field[BASE + x, t] for t in range(rows + 1))

    def along_y(here):
        side = here[rows]
        below = (pltpu.roll(jnp.where(row == 7, side, here[rows - 1]), 1, 0),) + here[: rows - 1]
        above = here[1:rows] + (pltpu.roll(jnp.where(row == 0, side, here[0]), 7, 0),)
        below += (pltpu.roll(jnp.where(row == 7, here[rows - 1], side), 1, 0),)
        above += (pltpu.roll(jnp.where(row == 0, here[0], side), 7, 0),)
        return below, above

    def sweep(k, start, count, reads=None):
        old, new = ((None, v1), (v1, v2), (v2, v3))[k]
        read = functools.partial(given, 0) if k == 0 else functools.partial(load, old)
        reads = start if k == 0 or reads is None else reads
        before, here = read(reads - 1), read(reads)
        for j in range(count):
            x = start + j
            after = read(reads + j + 1)
            term = given(k + 1, x)
            below, above = along_y(here)
            for t in range(rows + 1):
                around = (before[t] + after[t]) + (below[t] + above[t]) + 3.0 * here[t]
                value = term[t] + around * (1.0 / 9.0)
                value = value * keep if t == rows else value
                new[BASE + x, t] = value
            before, here = here, after

    def clear(field, start):
        for i in range(HALO):
            field[BASE + start + i] = jnp.zeros((rows + 1, 8, lanes), F32)

    def begin(i):
        for k, field in enumerate((v1, v2, v3)):
            sweep(k, i * STEP - 3 + k, 6 - 2 * k)
            if not inner and i == 0:
                pl.when(first)(functools.partial(clear, field, -HALO))

    def advance(i, at=None):
        at = i * STEP if at is None else at
        for k, field in enumerate((v1, v2, v3)):
            sweep(k, i * STEP + 3 - k, STEP, at + 3 - k)
            if not inner and i == steps - 1:
                pl.when(last)(functools.partial(clear, field, planes))
        x0 = i * STEP
        before, here = load(v3, at - 1), load(v3, at)
        for j in range(STEP):
            x = x0 + j
            after = load(v3, at + j + 1)
            below, above = along_y(here)
            for t in range(rows):
                down, up = along_z(here[t])
                potential_out[x, comb(t), :] = here[t] * (1.0 / 9.0)
                gradient_out[0, x, comb(t), :] = (after[t] - before[t]) * (0.5 / 9.0)
                gradient_out[1, x, comb(t), :] = (above[t] - below[t]) * (0.5 / 9.0)
                gradient_out[2, x, comb(t), :] = (up - down) * (0.5 / 9.0)
            before, here = here, after
        for copy in send(i):
            copy.start()
        return at + STEP

    if inner:
        begin(1)
        lax.fori_loop(1, steps - 1, advance, jnp.maximum(slab[0] - slabs, STEP))

        @pl.loop(1, steps - 1)
        def _(i):
            for copy in send(i):
                copy.wait()
    else:
        for i in (0, steps - 1):
            begin(i)
            advance(i)
        for i in (0, steps - 1):
            for copy in send(i):
                copy.wait()


def sweeps(inner, place, fields, y_faces, x_faces, results, slabs, pencils):
    planes, rows, _, lanes = fields[0].shape
    height = rows * 8
    ends = pltpu.VMEM((4, BASE + planes + BASE, 8, lanes), F32)
    field = pltpu.VMEM((BASE + planes + BASE, rows + 1, 8, lanes), F32)
    vmem, hbm = pl.BlockSpec(memory_space=pltpu.VMEM), pl.BlockSpec(memory_space=pl.ANY)
    scratch = [
        ends, field, field, field,
        pltpu.VMEM((planes, height, lanes), F32),
        pltpu.VMEM((3, planes, height, lanes), F32),
        pltpu.SemaphoreType.DMA((4,)),
    ]
    if not inner:
        scratch.append(pltpu.VMEM((4, 2 * HALO, rows, 8, lanes), F32))
    return pl.pallas_call(
        functools.partial(sweep_kernel, inner, slabs, pencils),
        out_shape=[
            jax.ShapeDtypeStruct((planes, height, lanes), F32),
            jax.ShapeDtypeStruct((3, planes, height, lanes), F32),
        ],
        in_specs=[pl.BlockSpec(memory_space=pltpu.SMEM)] * 2 + [vmem] * (6 + len(x_faces)) + [hbm] * len(results),
        out_specs=[hbm, hbm],
        scratch_shapes=scratch,
        input_output_aliases={} if inner else {10: 0, 11: 1},
        compiler_params=pltpu.CompilerParams(vmem_limit_bytes=28 << 20),
        cost_estimate=pl.CostEstimate(flops=1 << 25, bytes_accessed=(24 if inner else 4) << 20, transcendentals=0),
        name="inner_sweeps" if inner else "edge_sweeps",
    )(*place, *fields, *y_faces, *x_faces, *results)


def ring(values, axis, count):
    up = [(i, (i + 1) % count) for i in range(count)]
    down = [((i + 1) % count, i) for i in range(count)]
    low, high = values
    return lax.ppermute(high, axis, up), lax.ppermute(low, axis, down)


def on_device(fine, coarse, anchor, extent, owner, count):
    slabs, pencils = lax.axis_size("slab"), lax.axis_size("pencil")
    place = [lax.axis_index(name).astype(jnp.int32).reshape(1) for name in ("slab", "pencil")]
    sent = average(place, fine, anchor, extent, owner, count, slabs)
    received = lax.all_to_all(sent, "slab", split_axis=0, concat_axis=0, tiled=True)
    source, y_low, y_high = deposit(received, coarse)
    fields = prepare(source)
    y_low, y_high = ring((y_low, y_high), "pencil", pencils)

    x_low, x_high = ring(faces(fields[0], y_low, y_high), "slab", slabs)
    y_faces = (y_low, y_high)
    results = sweeps(True, place, fields, y_faces, (), (), slabs, pencils)
    potential, gradient = sweeps(False, place, fields, y_faces, (x_low, x_high), results, slabs, pencils)
    return potential, gradient


def solution(mesh):
    in_specs = (
        P("slab", "pencil", None, None, None, None),
        P("slab", "pencil", None),
        P("slab", "pencil", None, None),
        P("slab", "pencil", None, None),
        P("slab", "pencil", None, None),
        P("slab", "pencil"),
    )
    out_specs = (P("slab", "pencil", None), P(None, "slab", "pencil", None))
    return jax.shard_map(
        on_device, mesh=mesh, in_specs=in_specs, out_specs=out_specs, check_vma=False
    )
```

```python
import functools

import jax
import jax.numpy as jnp
from jax import lax
from jax.experimental import pallas as pl
from jax.experimental.pallas import tpu as pltpu
from jax.sharding import PartitionSpec as P

HALO = 4
META_ROWS = 8
STEP = 8
BASE = 8
GROUP = 16
DEEP = 4
F32 = jnp.float32


def average_kernel(slab, pencil, anchor, extent, owners, count, fine, sent, cells, sems):
    slots, fine_edge = cells.shape[:2]
    rows = sent.shape[1] - META_ROWS
    edge = fine_edge // 2
    lanes = sent.shape[2]
    groups = lanes // edge
    tiles = edge // groups
    share = 2 * groups

    def each_part(p, act):
        planes = extent[0, 0, 0, p]

        @pl.loop(0, jnp.minimum(lax.div(planes + share - 1, share), tiles))
        def _(tile):
            here = pl.ds(pl.multiple_of(tile * share, share), share)
            act(pltpu.make_async_copy(fine.at[0, 0, p, here], cells.at[p, here], sems.at[p]))

    live = jnp.minimum(count[0, 0], slots)

    @pl.loop(0, live)
    def _(p):
        each_part(p, lambda copy: copy.start())

    lane = lax.broadcasted_iota(jnp.int32, (META_ROWS, lanes), 1)
    source_lane = lax.broadcasted_iota(jnp.int32, (fine_edge, lanes), 0)
    target_lane = lax.broadcasted_iota(jnp.int32, (fine_edge, lanes), 1)
    for slot in range(sent.shape[0]):
        sent[slot, pl.ds(rows, META_ROWS), :] = jnp.zeros((META_ROWS, lanes), F32)

    @pl.loop(0, live)
    def _(p):
        each_part(p, lambda copy: copy.wait())
        owner = owners[0, 0, 0, p]
        total = jnp.zeros((rows, lanes), F32)
        for g in range(groups):
            pieces = [
                cells[p, pl.ds(2 * g + dx, tiles, stride=2 * groups), pl.ds(dy, edge, stride=2), :]
                for dx in range(2) for dy in range(2)
            ]
            part = ((pieces[0] + pieces[1]) + (pieces[2] + pieces[3])).reshape(rows, fine_edge)
            high = part.astype(jnp.bfloat16)
            low = (part - high.astype(F32)).astype(jnp.bfloat16)
            gather = jnp.where(target_lane == g * edge + source_lane // 2, 0.125, 0.0).astype(jnp.bfloat16)
            total = total + jnp.dot(high, gather, preferred_element_type=F32)
            total = total + jnp.dot(low, gather, preferred_element_type=F32)
        sent[owner, :rows, :] = total
        words = jnp.where(lane == 0, 1, 0)
        for d in range(3):
            words = jnp.where(lane == 1 + d, anchor[0, d, 0, p], words)
            words = jnp.where(lane == 4 + d, lax.shift_right_logical(extent[0, d, 0, p], 1), words)
        sent[owner, pl.ds(rows, META_ROWS), :] = words.astype(F32)


def average(place, fine, anchor, extent, owner, count, slabs):
    by_component = lambda a: jnp.transpose(a, (0, 3, 1, 2))
    slots, fine_edge = fine.shape[2], fine.shape[3]
    edge = fine_edge // 2
    rows = edge * edge * edge // 128
    smem = pl.BlockSpec(memory_space=pltpu.SMEM)
    return pl.pallas_call(
        average_kernel,
        out_shape=jax.ShapeDtypeStruct((slabs, rows + META_ROWS, 128), F32),
        in_specs=[smem] * 6 + [pl.BlockSpec(memory_space=pl.ANY)],
        out_specs=pl.BlockSpec(memory_space=pltpu.VMEM),
        scratch_shapes=[pltpu.VMEM(fine.shape[2:], F32), pltpu.SemaphoreType.DMA((slots,))],
        compiler_params=pltpu.CompilerParams(vmem_limit_bytes=56 << 20),
        name="average",
    )(*place, by_component(anchor), by_component(extent), by_component(owner), count, fine)


def deposit_kernel(received, coarse, source, y_low, y_high, words, sem):
    slabs, all_rows, lanes = received.shape
    rows = all_rows - META_ROWS
    edge = 32
    groups = lanes // edge
    planes, height, _ = source.shape
    for s in range(slabs):
        pltpu.make_async_copy(received.at[s, rows], words.at[s], sem).start()
    source[...] = jnp.zeros_like(source)
    for s in range(slabs):
        pltpu.make_async_copy(received.at[s, rows], words.at[s], sem).wait()
    row = lax.broadcasted_iota(jnp.int32, (edge, lanes), 0)
    lane = lax.broadcasted_iota(jnp.int32, (edge, lanes), 1)

    @pl.loop(0, slabs)
    def _(s):
        word = lambda k: words[s, k].astype(jnp.int32)

        @pl.when(word(0) > 0)
        def _():
            ax, ay, az, hx, hy, hz = (word(k) for k in range(1, 7))
            covered = (row < hy) & (lane >= az) & (lane < az + hz)
            here = pl.ds(ay, edge)

            @pl.loop(0, lax.div(hx + DEEP * groups - 1, DEEP * groups))
            def _(part):
                results = []
                for n in range(DEEP):
                    tile = part * DEEP + n
                    data = received[s, pl.ds(pl.multiple_of(tile * edge, edge), edge), :]
                    for g in range(groups):
                        i = tile * groups + g
                        x = ax + i
                        moved = pltpu.roll(data, lax.rem(az + lanes - g * edge, lanes), 1)
                        change = jnp.where(covered & (i < hx), moved - coarse[x, here, :], 0.0)
                        results.append((x, source[x, here, :] + change))
                for x, value in results:
                    source[x, here, :] = value

    row8 = lax.broadcasted_iota(jnp.int32, (2 * HALO, lanes), 0)

    @pl.loop(0, planes // 16)
    def _(part):
        for j in range(8):
            k = part * 8 + j
            for face, start, split in ((y_low, 0, HALO), (y_high, height - 2 * HALO, 0)):
                one, two = source[2 * k, start : start + 8, :], source[2 * k + 1, start : start + 8, :]
                if split:
                    face[k] = jnp.where(row8 < HALO, one, pltpu.roll(two, HALO, 0))
                else:
                    face[k] = jnp.where(row8 < HALO, pltpu.roll(one, HALO, 0), two)


def deposit(received, coarse):
    planes, height, lanes = coarse.shape
    face = jax.ShapeDtypeStruct((planes // 2, 2 * HALO, lanes), F32)
    vmem = pl.BlockSpec(memory_space=pltpu.VMEM)
    return pl.pallas_call(
        deposit_kernel,
        out_shape=[jax.ShapeDtypeStruct(coarse.shape, F32), face, face],
        in_specs=[vmem, vmem],
        out_specs=[vmem, vmem, vmem],
        scratch_shapes=[pltpu.SMEM((received.shape[0], lanes), F32), pltpu.SemaphoreType.DMA],
        compiler_params=pltpu.CompilerParams(vmem_limit_bytes=12 << 20),
        name="deposit",
    )(received, coarse)


def along_z(value):
    lanes = value.shape[1]
    lane = lax.broadcasted_iota(jnp.int32, value.shape, 1)
    down = jnp.where(lane == 0, 0.0, pltpu.roll(value, 1, 1))
    up = jnp.where(lane == lanes - 1, 0.0, pltpu.roll(value, lanes - 1, 1))
    return down, up


def z_terms(value):
    lanes = value.shape[1]
    lane = lax.broadcasted_iota(jnp.int32, value.shape, 1)
    down = [None] + [jnp.where(lane < d, 0.0, pltpu.roll(value, d, 1)) for d in (1, 2, 3)]
    up = [None] + [jnp.where(lane >= lanes - d, 0.0, pltpu.roll(value, lanes - d, 1)) for d in (1, 2, 3)]
    outer = (lane == 0) | (lane == lanes - 1)
    once = down[1] + up[1]
    twice = (down[2] + up[2]) + jnp.where(outer, 1.0, 2.0) * value
    thrice = (down[3] + up[3]) + (
        jnp.where((lane == 0) | (lane == lanes - 2), 2.0, 3.0) * up[1]
        + jnp.where((lane == 1) | (lane == lanes - 1), 2.0, 3.0) * down[1]
    )
    return (
        value,
        value + once * (1.0 / 3.0),
        value + (once * (2.0 / 9.0) + twice * (1.0 / 27.0)),
        (value + once * (1.0 / 9.0)) + (twice * (1.0 / 81.0) + thrice * (1.0 / 729.0)),
    )


def prepare_kernel(source, *fields):
    planes, height, _ = source.shape
    rows = height // 8

    @pl.loop(0, planes // GROUP)
    def _(k):
        for j in range(GROUP):
            for t in range(rows):
                for field, term in zip(fields, z_terms(source[GROUP * k + j, pl.ds(t, 8, stride=rows), :])):
                    field[GROUP * k + j, t] = term


def prepare(source):
    planes, height, lanes = source.shape
    field = jax.ShapeDtypeStruct((planes, height // 8, 8, lanes), F32)
    vmem = pl.BlockSpec(memory_space=pltpu.VMEM)
    return pl.pallas_call(
        prepare_kernel,
        out_shape=[field] * 4,
        in_specs=[vmem],
        out_specs=[vmem] * 4,
        compiler_params=pltpu.CompilerParams(vmem_limit_bytes=20 << 20),
        cost_estimate=pl.CostEstimate(flops=1 << 25, bytes_accessed=15 << 20, transcendentals=0),
        name="prepare",
    )(source)


def y_ends(low, high, half):
    row = lax.broadcasted_iota(jnp.int32, low.shape, 0)
    if half == 0:
        return jnp.where(row < HALO, high, pltpu.roll(low, HALO, 0))
    return jnp.where(row < HALO, pltpu.roll(high, HALO, 0), low)


def faces_kernel(field, y_low, y_high, x_low, x_high):
    planes, rows, _, _ = field.shape
    for face, start in ((x_low, 0), (x_high, planes - HALO)):
        for i in range(HALO):
            k, half = divmod(start + i, 2)
            for t in range(rows):
                face[i, t] = field[start + i, t]
            face[i, rows] = y_ends(y_low[k], y_high[k], half)


def faces(field, y_low, y_high):
    face = jax.ShapeDtypeStruct((HALO, field.shape[1] + 1) + field.shape[2:], F32)
    vmem = pl.BlockSpec(memory_space=pltpu.VMEM)
    return pl.pallas_call(
        faces_kernel,
        out_shape=[face, face],
        in_specs=[vmem] * 3,
        out_specs=[vmem] * 2,
        compiler_params=pltpu.CompilerParams(vmem_limit_bytes=4 << 20),
        name="faces",
    )(field, y_low, y_high)


def sweep_kernel(inner, slabs, pencils, slab, pencil, f0, f1, f2, f3, y_low, y_high, *rest):
    if inner:
        potential, gradient, *rest = rest
    else:
        x_low, x_high, _, _, potential, gradient, *rest = rest
    ends, v1, v2, v3, potential_out, gradient_out, sems, *rest = rest
    fields = (f0, f1, f2, f3)
    planes, rows, _, lanes = f0.shape
    height = rows * 8
    steps = planes // STEP
    first, last = slab[0] == 0, slab[0] == slabs - 1
    left, right = pencil[0] == 0, pencil[0] == pencils - 1
    row = lax.broadcasted_iota(jnp.int32, (8, lanes), 0)
    keep = jnp.where((right & (row < HALO)) | (left & (row >= HALO)), 0.0, 1.0)

    def send(i):
        here = pl.ds(i * STEP, STEP)
        copies = [pltpu.make_async_copy(potential_out.at[here], potential.at[here], sems.at[0])]
        for d in range(3):
            copies.append(pltpu.make_async_copy(gradient_out.at[d, here], gradient.at[d, here], sems.at[1 + d]))
        return copies

    def comb(t):
        return pl.ds(t, 8, stride=rows)

    def set_ends(x, value):
        for k, term in enumerate(z_terms(value)):
            ends[k, BASE + x] = term

    def set_y_faces(k):
        low, high = y_low[k], y_high[k]
        for half in range(2):
            set_ends(2 * k + half, y_ends(low, high, half) * keep)

    if inner:
        @pl.loop(0, planes // 16)
        def _(k):
            for j in range(8):
                set_y_faces(8 * k + j)
    else:
        for j in range(8):
            set_y_faces(j)
            set_y_faces(planes // 2 - 1 - j)
        (beyond,) = rest
        for i in range(HALO):
            for edge, x, face in ((first, i - HALO, x_low), (last, planes + i, x_high)):
                scale = jnp.where(edge, 0.0, 1.0)
                for t in range(rows):
                    for k, term in enumerate(z_terms(face[i, t] * scale)):
                        beyond[k, x % (2 * HALO), t] = term
                set_ends(x, face[i, rows] * (keep * scale))

    def given(k, x):
        if isinstance(x, int) and not 0 <= x < planes:
            return tuple(beyond[k, x % (2 * HALO), t] for t in range(rows)) + (ends[k, BASE + x],)
        return tuple(fields[k][x, t] for t in range(rows)) + (ends[k, BASE + x],)

    def load(field, x):
        return tuple(field[BASE + x, t] for t in range(rows + 1))

    def along_y(here):
        side = here[rows]
        below = (pltpu.roll(jnp.where(row == 7, side, here[rows - 1]), 1, 0),) + here[: rows - 1]
        above = here[1:rows] + (pltpu.roll(jnp.where(row == 0, side, here[0]), 7, 0),)
        below += (pltpu.roll(jnp.where(row == 7, here[rows - 1], side), 1, 0),)
        above += (pltpu.roll(jnp.where(row == 0, here[0], side), 7, 0),)
        return below, above

    def sweep(k, start, count, reads=None):
        old, new = ((None, v1), (v1, v2), (v2, v3))[k]
        read = functools.partial(given, 0) if k == 0 else functools.partial(load, old)
        reads = start if k == 0 or reads is None else reads
        before, here = read(reads - 1), read(reads)
        for j in range(count):
            x = start + j
            after = read(reads + j + 1)
            term = given(k + 1, x)
            below, above = along_y(here)
            for t in range(rows + 1):
                around = (before[t] + after[t]) + (below[t] + above[t]) + 3.0 * here[t]
                value = term[t] + around * (1.0 / 9.0)
                value = value * keep if t == rows else value
                new[BASE + x, t] = value
            before, here = here, after

    def clear(field, start):
        for i in range(HALO):
            field[BASE + start + i] = jnp.zeros((rows + 1, 8, lanes), F32)

    def begin(i):
        for k, field in enumerate((v1, v2, v3)):
            sweep(k, i * STEP - 3 + k, 6 - 2 * k)
            if not inner and i == 0:
                pl.when(first)(functools.partial(clear, field, -HALO))

    def advance(i, at=None):
        at = i * STEP if at is None else at
        for k, field in enumerate((v1, v2, v3)):
            sweep(k, i * STEP + 3 - k, STEP, at + 3 - k)
            if not inner and i == steps - 1:
                pl.when(last)(functools.partial(clear, field, planes))
        x0 = i * STEP
        before, here = load(v3, at - 1), load(v3, at)
        for j in range(STEP):
            x = x0 + j
            after = load(v3, at + j + 1)
            below, above = along_y(here)
            for t in range(rows):
                down, up = along_z(here[t])
                potential_out[x, comb(t), :] = here[t] * (1.0 / 9.0)
                gradient_out[0, x, comb(t), :] = (after[t] - before[t]) * (0.5 / 9.0)
                gradient_out[1, x, comb(t), :] = (above[t] - below[t]) * (0.5 / 9.0)
                gradient_out[2, x, comb(t), :] = (up - down) * (0.5 / 9.0)
            before, here = here, after
        for copy in send(i):
            copy.start()
        return at + STEP

    if inner:
        begin(1)
        lax.fori_loop(1, steps - 1, advance, jnp.maximum(slab[0] - slabs, STEP))

        @pl.loop(1, steps - 1)
        def _(i):
            for copy in send(i):
                copy.wait()
    else:
        for i in (0, steps - 1):
            begin(i)
            advance(i)
        for i in (0, steps - 1):
            for copy in send(i):
                copy.wait()


def sweeps(inner, place, fields, y_faces, x_faces, results, slabs, pencils):
    planes, rows, _, lanes = fields[0].shape
    height = rows * 8
    ends = pltpu.VMEM((4, BASE + planes + BASE, 8, lanes), F32)
    field = pltpu.VMEM((BASE + planes + BASE, rows + 1, 8, lanes), F32)
    vmem, hbm = pl.BlockSpec(memory_space=pltpu.VMEM), pl.BlockSpec(memory_space=pl.ANY)
    scratch = [
        ends, field, field, field,
        pltpu.VMEM((planes, height, lanes), F32),
        pltpu.VMEM((3, planes, height, lanes), F32),
        pltpu.SemaphoreType.DMA((4,)),
    ]
    if not inner:
        scratch.append(pltpu.VMEM((4, 2 * HALO, rows, 8, lanes), F32))
    return pl.pallas_call(
        functools.partial(sweep_kernel, inner, slabs, pencils),
        out_shape=[
            jax.ShapeDtypeStruct((planes, height, lanes), F32),
            jax.ShapeDtypeStruct((3, planes, height, lanes), F32),
        ],
        in_specs=[pl.BlockSpec(memory_space=pltpu.SMEM)] * 2 + [vmem] * (6 + len(x_faces)) + [hbm] * len(results),
        out_specs=[hbm, hbm],
        scratch_shapes=scratch,
        input_output_aliases={} if inner else {10: 0, 11: 1},
        compiler_params=pltpu.CompilerParams(vmem_limit_bytes=28 << 20),
        cost_estimate=pl.CostEstimate(flops=1 << 25, bytes_accessed=(24 if inner else 4) << 20, transcendentals=0),
        name="inner_sweeps" if inner else "edge_sweeps",
    )(*place, *fields, *y_faces, *x_faces, *results)


def ring(values, axis, count):
    up = [(i, (i + 1) % count) for i in range(count)]
    down = [((i + 1) % count, i) for i in range(count)]
    low, high = values
    return lax.ppermute(high, axis, up), lax.ppermute(low, axis, down)


def on_device(fine, coarse, anchor, extent, owner, count):
    slabs, pencils = lax.axis_size("slab"), lax.axis_size("pencil")
    place = [lax.axis_index(name).astype(jnp.int32).reshape(1) for name in ("slab", "pencil")]
    sent = average(place, fine, anchor, extent, owner, count, slabs)
    received = lax.all_to_all(sent, "slab", split_axis=0, concat_axis=0, tiled=True)
    source, y_low, y_high = deposit(received, coarse)
    fields = prepare(source)
    y_low, y_high = ring((y_low, y_high), "pencil", pencils)

    x_low, x_high = ring(faces(fields[0], y_low, y_high), "slab", slabs)
    y_faces = (y_low, y_high)
    results = sweeps(True, place, fields, y_faces, (), (), slabs, pencils)
    potential, gradient = sweeps(False, place, fields, y_faces, (x_low, x_high), results, slabs, pencils)
    return potential, gradient


def solution(mesh):
    in_specs = (
        P("slab", "pencil", None, None, None, None),
        P("slab", "pencil", None),
        P("slab", "pencil", None, None),
        P("slab", "pencil", None, None),
        P("slab", "pencil", None, None),
        P("slab", "pencil"),
    )
    out_specs = (P("slab", "pencil", None), P(None, "slab", "pencil", None))
    return jax.shard_map(
        on_device, mesh=mesh, in_specs=in_specs, out_specs=out_specs, check_vma=False
    )
```
